128 devices in a mesh: seq: 16 (over y_hi, z, core), res: 8 (over x, y_lo).
Axes of the slice: x: 4, y: 4 (y_hi: 2, y_lo: 2; y = y_hi * 2 + y_lo), z: 4, core: 2. Of those that a mesh axis runs over, the one named last changes fastest.
Arguments:
- alignment_features: bfloat16 [64, 1024, 256], P('seq', 'res'), may hold values from -6 to 40
- alignment_standardize_gain: float32 [256], replicated, may hold values from 0.75 to 1.25
- stacked_qkvg_matrix: bfloat16 [256, 1024], replicated, may hold values from -1.65 to 1.65
- sigmoid_shift_vector: float32 [256], replicated, may hold values from -4 to 4
- final_linear_matrix: bfloat16 [256, 256], replicated, may hold values from -0.375 to 0.375
- pairwise_features: bfloat16 [1024, 1024, 128], P('seq', 'res'), may hold values from -6 to 6
- pairwise_standardize_gain: float32 [128], replicated, may hold values from 0.5 to 1.5
- pairterm_linear_matrix: bfloat16 [128, 8], replicated, may hold values from -0.5 to 0.5
- upstream_derivative: bfloat16 [64, 1024, 256], P('seq', 'res'), may hold values from -6 to 6
Outputs:
- alignment_increment: bfloat16 [64, 1024, 256], P('seq', 'res')
- derivative_of_alignment: bfloat16 [64, 1024, 256], P('seq', 'res')
- derivative_of_pairwise: bfloat16 [1024, 1024, 128], P('seq', 'res')
- derivative_of_stacked_matrix: float32 [256, 1024], replicated
- derivative_of_final_matrix: float32 [256, 256], replicated
- derivative_of_pairterm_matrix: float32 [128, 8], replicated
The draws below stay inside these ranges and needn't reach their ends.
All inputs are finite; a program needn't handle non-finite values.
Results may differ from the reference program's by a relative error of at most 0.022.
Values may be sent and summed in bfloat16 or wider, within the bound.
No kernel may reach another device: no remote copies, remote signals or barrier semaphores. Data moves between devices by JAX's collectives and lax.ppermute only.
A program may use at most 128 MiB of HBM per device.

```python
import jax
import jax.numpy as jnp
from jax import lax

ALIGNMENT_WIDTH = 256
HEADS = 8
DH = 32
C_PAIR = 128
S_DEV = 4
ALIGNED_TOTAL = 64
AMINO_TOTAL = 1024
TOTAL_HEAD_WIDTH = 256
PAIR_ROWS = 64
N_SEQ = 16


def draw_alignment_features(key, part):
    key = jax.random.fold_in(key, 1)
    seed_stochastic_handle = jax.random.fold_in(key, 0)
    content_vectors = jnp.clip(jax.random.normal(seed_stochastic_handle, (ALIGNED_TOTAL, AMINO_TOTAL, ALIGNMENT_WIDTH), jnp.float32), -6.0, 6.0)
    return content_vectors.astype(jnp.bfloat16)


def draw_stacked_qkvg_matrix(key, part):
    key = jax.random.fold_in(key, 2)
    seed_stochastic_handle = jax.random.fold_in(key, 0)
    softmax_probabilities = jnp.clip(jax.random.normal(seed_stochastic_handle, (ALIGNMENT_WIDTH, 4 * TOTAL_HEAD_WIDTH), jnp.float32), -6.0, 6.0) * ALIGNMENT_WIDTH ** (-0.5)
    return softmax_probabilities.astype(jnp.bfloat16)


def level_of(key, extent, cuts, low, high):
    factor_of = 1.0
    for position, shards_of in cuts:
        draws = jax.random.uniform(jax.random.fold_in(jax.random.fold_in(key, 6), position), (shards_of,), jnp.float32, low / len(cuts), high / len(cuts))
        factor_of = factor_of * jnp.repeat(jnp.exp(draws), extent[position] // shards_of).reshape((-1,) + (1,) * (len(extent) - 1 - position))
    return factor_of


def normal_values(key, dims, width, reach, shards=(), held_as=jnp.bfloat16):
    loudness = level_of(key, dims, shards, -0.22, 0.18) if shards else 1.0
    values = jax.random.normal(key, dims, jnp.float32) * width * loudness
    return jnp.minimum(jnp.maximum(values, -reach), reach).astype(held_as)


def setup_inputs(seed: int = 0) -> dict:
    seeds = jax.random.split(jax.random.key(seed), 10)
    return {
        "alignment_features": draw_alignment_features(jax.random.fold_in(seeds[9], 71), 0),
        "alignment_standardize_gain": jnp.clip(1.0 + 0.05 * jax.random.normal(seeds[1], (ALIGNMENT_WIDTH,), jnp.float32), 0.75, 1.25),
        "stacked_qkvg_matrix": draw_stacked_qkvg_matrix(jax.random.fold_in(seeds[9], 71), 0),
        "sigmoid_shift_vector": normal_values(seeds[3], (TOTAL_HEAD_WIDTH,), 1.0, 4.0, (), jnp.float32),
        "final_linear_matrix": normal_values(seeds[4], (TOTAL_HEAD_WIDTH, ALIGNMENT_WIDTH), TOTAL_HEAD_WIDTH ** -0.5, 0.375),
        "pairwise_features": normal_values(seeds[5], (AMINO_TOTAL, AMINO_TOTAL, C_PAIR), 1.0, 6.0, ((0, 16), (1, 8))),
        "pairwise_standardize_gain": jnp.clip(1.0 + 0.1 * jax.random.normal(seeds[6], (C_PAIR,), jnp.float32), 0.5, 1.5),
        "pairterm_linear_matrix": normal_values(seeds[7], (C_PAIR, HEADS), C_PAIR ** -0.5, 0.5),
        "upstream_derivative": normal_values(seeds[8], (ALIGNED_TOTAL, AMINO_TOTAL, ALIGNMENT_WIDTH), 1.0, 6.0, ((0, 16), (1, 8))),
    }


NORM_EPSILON = 1e-05

def standardize_apply(content_vectors, norm_gain):
    content_vectors = content_vectors.astype(jnp.float32)
    average = lax.optimization_barrier(jnp.mean(content_vectors, axis=-1, keepdims=True))
    centered = content_vectors - average
    inv_std = lax.rsqrt(lax.optimization_barrier(jnp.mean(centered * centered, axis=-1, keepdims=True)) + NORM_EPSILON)
    norm_hat = centered * inv_std
    return (norm_hat, inv_std, (norm_hat * norm_gain).astype(jnp.bfloat16))

def standardize_derivative(norm_hat, inv_std, norm_gain, grad_out):
    d_hat = grad_out * norm_gain
    mean_d = lax.optimization_barrier(jnp.mean(d_hat, axis=-1, keepdims=True))
    mean_dx = lax.optimization_barrier(jnp.mean(d_hat * norm_hat, axis=-1, keepdims=True))
    return inv_std * (d_hat - mean_d - norm_hat * mean_dx)

def round_low(content_vectors):
    return lax.optimization_barrier(content_vectors.astype(jnp.bfloat16)).astype(jnp.float32)

def upcast_to_float32(content_vectors):
    return content_vectors.astype(jnp.float32)

def softmax_rows(q_one, k_one, bias_ij):
    scores = jnp.einsum('ihd,jhd->hij', upcast_to_float32(q_one), upcast_to_float32(k_one)) + bias_ij
    row_max = lax.optimization_barrier(jnp.max(scores, axis=-1, keepdims=True))
    exp_scores = jnp.exp(scores - row_max)
    row_sum = lax.optimization_barrier(jnp.sum(exp_scores, axis=-1, keepdims=True))
    return exp_scores / row_sum

def split_blocks(array):
    return array.reshape((N_SEQ, S_DEV) + array.shape[1:])

def reference(alignment_features, alignment_standardize_gain, stacked_qkvg_matrix, sigmoid_shift_vector, final_linear_matrix, pairwise_features, pairwise_standardize_gain, pairterm_linear_matrix, upstream_derivative):
    head_scale = DH ** (-0.5)
    alignment_centered_unitless, alignment_reciprocal_spread, alignment_after_standardize = standardize_apply(alignment_features, alignment_standardize_gain)
    linear_mapped_lines = jnp.einsum('esc,cw->esw', upcast_to_float32(alignment_after_standardize), upcast_to_float32(stacked_qkvg_matrix))
    queries = (linear_mapped_lines[..., :TOTAL_HEAD_WIDTH] * head_scale).astype(jnp.bfloat16)
    keys = linear_mapped_lines[..., TOTAL_HEAD_WIDTH:2 * TOTAL_HEAD_WIDTH].astype(jnp.bfloat16)
    content_vectors = linear_mapped_lines[..., 2 * TOTAL_HEAD_WIDTH:3 * TOTAL_HEAD_WIDTH].astype(jnp.bfloat16)
    gate_vals = jax.nn.sigmoid(linear_mapped_lines[..., 3 * TOTAL_HEAD_WIDTH:] + sigmoid_shift_vector)
    pair_blocks = pairwise_features.reshape(N_SEQ, PAIR_ROWS, AMINO_TOTAL, C_PAIR)

    def bias_block(pair_block):
        unused_hat, unused_inv, pair_normed = standardize_apply(pair_block, pairwise_standardize_gain)
        return jnp.einsum('jic,ch->hji', upcast_to_float32(pair_normed), upcast_to_float32(pairterm_linear_matrix)).astype(jnp.bfloat16)
    bias_ji = jnp.moveaxis(lax.map(bias_block, pair_blocks), 0, 1).reshape(HEADS, AMINO_TOTAL, AMINO_TOTAL)
    bias_ij = upcast_to_float32(jnp.swapaxes(bias_ji, 1, 2))
    q_heads = queries.reshape(ALIGNED_TOTAL, AMINO_TOTAL, HEADS, DH)
    k_heads = keys.reshape(ALIGNED_TOTAL, AMINO_TOTAL, HEADS, DH)
    v_heads = content_vectors.reshape(ALIGNED_TOTAL, AMINO_TOTAL, HEADS, DH)

    def forward_one(inputs):
        q_one, k_one, v_one = inputs
        prob_full = softmax_rows(q_one, k_one, bias_ij)
        return jnp.einsum('hij,jhd->ihd', round_low(prob_full), upcast_to_float32(v_one))
    attended = lax.map(forward_one, (q_heads, k_heads, v_heads)).reshape(ALIGNED_TOTAL, AMINO_TOTAL, TOTAL_HEAD_WIDTH)
    gated_out = (gate_vals * attended).astype(jnp.bfloat16)
    alignment_increment = jnp.einsum('srk,kc->src', upcast_to_float32(gated_out), upcast_to_float32(final_linear_matrix)).astype(jnp.bfloat16)
    derivative_of_final_matrix = jnp.einsum('srk,src->kc', upcast_to_float32(gated_out), upcast_to_float32(upstream_derivative))
    d_gated = jnp.einsum('src,kc->srk', upcast_to_float32(upstream_derivative), upcast_to_float32(final_linear_matrix))
    d_att = (d_gated * gate_vals).astype(jnp.bfloat16)
    d_gate_pre = d_gated * attended * gate_vals * (1.0 - gate_vals)
    datt_heads = d_att.reshape(ALIGNED_TOTAL, AMINO_TOTAL, HEADS, DH)

    def seq_step(running, inputs):
        q_one, k_one, v_one, datt_one = inputs
        prob_full = softmax_rows(q_one, k_one, bias_ij)
        d_probs = jnp.einsum('ihd,jhd->hij', upcast_to_float32(datt_one), upcast_to_float32(v_one))
        row_dot = lax.optimization_barrier(jnp.sum(prob_full * d_probs, axis=-1, keepdims=True))
        d_scores = round_low(prob_full * (d_probs - row_dot))
        d_query = jnp.einsum('hij,jhd->ihd', d_scores, upcast_to_float32(k_one)) * head_scale
        d_key = jnp.einsum('hij,ihd->jhd', d_scores, upcast_to_float32(q_one))
        d_value = jnp.einsum('hij,ihd->jhd', round_low(prob_full), upcast_to_float32(datt_one))
        return (running + d_scores, (d_query, d_key, d_value))

    def block_step(running, block_inputs):
        block_sum, outputs = lax.scan(seq_step, jnp.zeros((HEADS, AMINO_TOTAL, AMINO_TOTAL), jnp.float32), block_inputs)
        return (running + round_low(block_sum), outputs)
    d_bias_ij, (d_queries, d_keys, d_values) = lax.scan(block_step, jnp.zeros((HEADS, AMINO_TOTAL, AMINO_TOTAL), jnp.float32), (split_blocks(q_heads), split_blocks(k_heads), split_blocks(v_heads), split_blocks(datt_heads)))
    derivative_of_mapped = jnp.concatenate((d_queries.reshape(ALIGNED_TOTAL, AMINO_TOTAL, TOTAL_HEAD_WIDTH), d_keys.reshape(ALIGNED_TOTAL, AMINO_TOTAL, TOTAL_HEAD_WIDTH), d_values.reshape(ALIGNED_TOTAL, AMINO_TOTAL, TOTAL_HEAD_WIDTH), d_gate_pre), axis=-1).astype(jnp.bfloat16)
    derivative_of_stacked_matrix = jnp.einsum('kde,kdh->eh', upcast_to_float32(alignment_after_standardize), upcast_to_float32(derivative_of_mapped))
    derivative_of_standardized_alignment = jnp.einsum('njr,kr->njk', upcast_to_float32(derivative_of_mapped), upcast_to_float32(stacked_qkvg_matrix))
    derivative_of_alignment = standardize_derivative(alignment_centered_unitless, alignment_reciprocal_spread, alignment_standardize_gain, derivative_of_standardized_alignment).astype(jnp.bfloat16)
    d_bias_blocks = jnp.moveaxis(jnp.swapaxes(d_bias_ij, 1, 2).reshape(HEADS, N_SEQ, PAIR_ROWS, AMINO_TOTAL), 1, 0)

    def pair_back(inputs):
        pair_block, bias_grad = inputs
        pair_hat, pair_inv, pair_normed = standardize_apply(pair_block, pairwise_standardize_gain)
        d_pair_normed = jnp.einsum('hji,ch->jic', bias_grad, upcast_to_float32(pairterm_linear_matrix), precision=lax.Precision.HIGHEST)
        d_block = standardize_derivative(pair_hat, pair_inv, pairwise_standardize_gain, d_pair_normed).astype(jnp.bfloat16)
        d_weight = jnp.einsum('jic,hji->ch', upcast_to_float32(pair_normed), bias_grad, precision=lax.Precision.HIGHEST)
        return (d_block, d_weight)
    d_pair_blocks, d_weight_parts = lax.map(pair_back, (pair_blocks, d_bias_blocks))
    derivative_of_pairwise = d_pair_blocks.reshape(AMINO_TOTAL, AMINO_TOTAL, C_PAIR)
    derivative_of_pairterm_matrix = lax.optimization_barrier(jnp.sum(d_weight_parts, axis=0))
    return (alignment_increment, derivative_of_alignment, derivative_of_pairwise, derivative_of_stacked_matrix, derivative_of_final_matrix, derivative_of_pairterm_matrix)
```

```python
import functools

import jax
import jax.numpy as jnp
from jax import lax
from jax.experimental import pallas as pl
from jax.experimental.pallas import tpu as pltpu
from jax.sharding import PartitionSpec as P

EPS = 1e-05
F32 = jnp.float32
BF16 = jnp.bfloat16
HEADS = 8
DH = 32
SCALE = DH ** (-0.5)
VMEM = 48 * 1024 * 1024


def nn(a, b):
    return lax.dot_general(a, b, (((1,), (0,)), ((), ())), preferred_element_type=F32)


def nt(a, b):
    return lax.dot_general(a, b, (((1,), (1,)), ((), ())), preferred_element_type=F32)


def tn(a, b):
    return lax.dot_general(a, b, (((0,), (0,)), ((), ())), preferred_element_type=F32)


def normalize(x):
    x = x.astype(F32)
    centered = x - jnp.mean(x, axis=-1, keepdims=True)
    inv = lax.rsqrt(jnp.mean(centered * centered, axis=-1, keepdims=True) + EPS)
    return centered * inv, inv


def normalize_grad(hat, inv, gain, grad):
    g = grad * gain
    mean_g = jnp.mean(g, axis=-1, keepdims=True)
    mean_gx = jnp.mean(g * hat, axis=-1, keepdims=True)
    return inv * (g - mean_g - hat * mean_gx)


def params(n=1):
    return pltpu.CompilerParams(
        dimension_semantics=("arbitrary",) * n, vmem_limit_bytes=VMEM
    )


def project_kernel(x_ref, gain_ref, w_ref, shift_ref, wo_ref, up_ref, pack_ref, gate_ref, dg_ref):
    hat, _ = normalize(x_ref[0])
    normed = (hat * gain_ref[...]).astype(BF16)
    proj = nn(normed, w_ref[...])
    q = (proj[:, :256] * SCALE).astype(BF16)
    k = proj[:, 256:512].astype(BF16)
    v = proj[:, 512:768].astype(BF16)
    gate = jax.nn.sigmoid(proj[:, 768:] + shift_ref[...])
    d_gated = nt(up_ref[0], wo_ref[...])
    da = (d_gated * gate).astype(BF16)
    gate_ref[0] = gate
    dg_ref[0] = d_gated
    for h in range(HEADS):
        c = slice(h * DH, (h + 1) * DH)
        pack_ref[h, 0] = jnp.concatenate([q[:, c], k[:, c], v[:, c], da[:, c]], axis=1)


def project(x, gain, w, shift, wo, up):
    s, n, c = x.shape
    whole = lambda *shape: pl.BlockSpec(shape, lambda i: (0,) * len(shape))
    row = pl.BlockSpec((1, n, c), lambda i: (i, 0, 0))
    return pl.pallas_call(
        project_kernel,
        grid=(s,),
        in_specs=[row, whole(1, c), whole(c, 4 * c), whole(1, c), whole(c, c), row],
        out_specs=[pl.BlockSpec((HEADS, 1, n, 128), lambda i: (0, i, 0, 0)), row, row],
        out_shape=[
            jax.ShapeDtypeStruct((HEADS, s, n, 128), BF16),
            jax.ShapeDtypeStruct((s, n, c), F32),
            jax.ShapeDtypeStruct((s, n, c), F32),
        ],
        compiler_params=params(),
        name="project",
    )(x, gain, w, shift, wo, up)


def bias_kernel(x_ref, gain_ref, wt_ref, out_ref, tmp):
    wt = wt_ref[...]
    for j in range(x_ref.shape[0]):
        hat, _ = normalize(x_ref[j])
        normed = (hat * gain_ref[...]).astype(BF16)
        tmp[:, j, :] = nt(wt, normed)
    out_ref[...] = tmp[...].astype(BF16)


def pair_bias(pair, gain, wt):
    j, i, c = pair.shape
    step = 16
    return pl.pallas_call(
        bias_kernel,
        grid=(j // step,),
        in_specs=[
            pl.BlockSpec((step, i, c), lambda g: (g, 0, 0)),
            pl.BlockSpec((1, c), lambda g: (0, 0)),
            pl.BlockSpec((HEADS, c), lambda g: (0, 0)),
        ],
        out_specs=pl.BlockSpec((HEADS, step, i), lambda g: (0, g, 0)),
        out_shape=jax.ShapeDtypeStruct((HEADS, j, i), BF16),
        scratch_shapes=[pltpu.VMEM((HEADS, step, i), F32)],
        compiler_params=params(),
        name="pair_bias",
    )(pair, gain, wt)


def attention_kernel(x_ref, b_ref, o_ref, db_ref, xt, acc, scores, exps, dsc, rq, ra, delta):
    step = pl.program_id(0)
    n_seq = x_ref.shape[1]
    iw = 256
    zeros = lambda rows: jnp.zeros((rows, iw), BF16)

    @pl.when(step == 0)
    def _():
        for s in range(n_seq):
            for r in range(8):
                xt[s, :, r * 128 : (r + 1) * 128] = x_ref[r, s].T
        acc[...] = jnp.zeros_like(acc)

    cols = pl.ds(pl.multiple_of(step * iw, iw), iw)
    ones = jnp.ones((16, 1024), BF16)
    for s in range(n_seq):
        rhs_q = jnp.concatenate([zeros(32), xt[s, 0:32, cols], zeros(64)], axis=0)
        rq[s] = rhs_q
        top = jnp.full((8, iw), -jnp.inf, F32)
        for c in range(8):
            lo = b_ref[2 * c : 2 * c + 2, 0].reshape(128, 128)
            hi = b_ref[2 * c : 2 * c + 2, 1].reshape(128, 128)
            sc = nn(x_ref[c, s], rhs_q) + jnp.concatenate([lo, hi], axis=1).astype(F32)
            scores[c] = sc
            top = jnp.maximum(top, jnp.max(sc.reshape(16, 8, iw), axis=0))
        top = jnp.max(top, axis=0, keepdims=True)
        for c in range(8):
            exps[s, c] = jnp.exp(scores[c] - top).astype(BF16)
        left = jnp.concatenate([xt[s, 64:96, :], ones], axis=0)
        ot = nn(left, exps[s].reshape(1024, iw))
        inv = 1.0 / ot[32:33]
        ot = ot[0:32] * inv
        da = (xt[s, 96:128, cols].astype(F32) * inv).astype(BF16)
        delta[s] = jnp.sum(da.astype(F32) * ot, axis=0, keepdims=True)
        ra[s] = jnp.concatenate([zeros(64), da, zeros(32)], axis=0)
        for t in range(2):
            part = jnp.concatenate(
                [ot[:, t * 128 : (t + 1) * 128], jnp.zeros((96, 128), F32)], axis=0
            )
            acc[s, step * 2 + t] += part.T
    for c in range(8):
        total = jnp.zeros((128, iw), F32)
        for s in range(n_seq):
            e = exps[s, c]
            ds = e.astype(F32) * (nn(x_ref[c, s], ra[s]) - delta[s])
            total = total + ds
            ds = ds.astype(BF16)
            dsc[s, c] = ds
            acc[s, c] += nt(ds, rq[s]) + nt(e, ra[s])
        low = total.astype(BF16)
        db_ref[2 * c : 2 * c + 2, 0] = low[:, :128].reshape(2, 64, 128)
        db_ref[2 * c : 2 * c + 2, 1] = low[:, 128:].reshape(2, 64, 128)
    for s in range(n_seq):
        dq = nn(xt[s, 32:64, :], dsc[s].reshape(1024, iw)) * SCALE
        for t in range(2):
            part = jnp.concatenate(
                [jnp.zeros((96, 128), F32), dq[:, t * 128 : (t + 1) * 128]], axis=0
            )
            acc[s, step * 2 + t] += part.T

    @pl.when(step == pl.num_programs(0) - 1)
    def _():
        for s in range(n_seq):
            for r in range(8):
                o_ref[r, s] = acc[s, r].astype(BF16)


def attention(x, bias):
    r, s, n, _ = x.shape
    seqs = bias.shape[0]
    return pl.pallas_call(
        attention_kernel,
        grid=(4,),
        in_specs=[
            pl.BlockSpec((r, s, n, 128), lambda g: (0, 0, 0, 0)),
            pl.BlockSpec((seqs, 2, 64, 128), lambda g: (0, g, 0, 0)),
        ],
        out_specs=[
            pl.BlockSpec((r, s, n, 128), lambda g: (0, 0, 0, 0)),
            pl.BlockSpec((seqs, 2, 64, 128), lambda g: (0, g, 0, 0)),
        ],
        out_shape=[
            jax.ShapeDtypeStruct((r, s, n, 128), BF16),
            jax.ShapeDtypeStruct((seqs, r, 64, 128), BF16),
        ],
        scratch_shapes=[
            pltpu.VMEM((s, 128, 1024), BF16),
            pltpu.VMEM((s, 8, 128, 128), F32),
            pltpu.VMEM((8, 128, 256), F32),
            pltpu.VMEM((s, 8, 128, 256), BF16),
            pltpu.VMEM((s, 8, 128, 256), BF16),
            pltpu.VMEM((s, 128, 256), BF16),
            pltpu.VMEM((s, 128, 256), BF16),
            pltpu.VMEM((s, 1, 256), F32),
        ],
        compiler_params=params(),
        name="attention",
    )(x, bias)


def finish_kernel(
    x_ref, gain_ref, w_ref, wo_ref, up_ref, gate_ref, dg_ref, back_ref,
    inc_ref, dx_ref, dw_ref, acc,
):
    step = pl.program_id(0)
    hat, inv = normalize(x_ref[0])
    gain = gain_ref[...]
    normed = (hat * gain).astype(BF16)
    gate = gate_ref[0]
    d_gated = dg_ref[0]
    up = up_ref[0]
    back = [back_ref[h, 0] for h in range(HEADS)]
    pick = lambda a: jnp.concatenate([b[:, a * DH : (a + 1) * DH] for b in back], axis=1)
    attended = pick(0).astype(F32)
    gated = (gate * attended).astype(BF16)
    inc_ref[0] = nn(gated, wo_ref[...]).astype(BF16)
    d_pre = (d_gated * attended * gate * (1.0 - gate)).astype(BF16)
    d_proj = jnp.concatenate([pick(3), pick(1), pick(2), d_pre], axis=1)
    grad = nt(d_proj, w_ref[...])
    dx_ref[0] = normalize_grad(hat, inv, gain, grad).astype(BF16)

    @pl.when(step == 0)
    def _():
        acc[...] = jnp.zeros_like(acc)

    acc[:, :1024] += tn(normed, d_proj)
    acc[:, 1024:] += tn(gated, up)

    @pl.when(step == pl.num_programs(0) - 1)
    def _():
        for b in range(10):
            dw_ref[b] = acc[:, b * 128 : (b + 1) * 128].astype(BF16)


def finish(x, gain, w, wo, up, gate, dg, back):
    s, n, c = x.shape
    whole = lambda *shape: pl.BlockSpec(shape, lambda i: (0,) * len(shape))
    row = pl.BlockSpec((1, n, c), lambda i: (i, 0, 0))
    return pl.pallas_call(
        finish_kernel,
        grid=(s,),
        in_specs=[
            row, whole(1, c), whole(c, 4 * c), whole(c, c), row, row, row,
            pl.BlockSpec((HEADS, 1, n, 128), lambda i: (0, i, 0, 0)),
        ],
        out_specs=[row, row, whole(10, 256, 128)],
        out_shape=[
            jax.ShapeDtypeStruct((s, n, c), BF16),
            jax.ShapeDtypeStruct((s, n, c), BF16),
            jax.ShapeDtypeStruct((10, 256, 128), BF16),
        ],
        scratch_shapes=[pltpu.VMEM((c, 5 * c), F32)],
        compiler_params=params(),
        name="finish",
    )(x, gain, w, wo, up, gate, dg, back)


def pair_grad_kernel(x_ref, gain_ref, wt_ref, db_ref, dx_ref, dw_ref, tmp):
    step = pl.program_id(0)
    gain = gain_ref[...]
    wt = wt_ref[...]
    tmp[...] = db_ref[...].astype(F32)

    @pl.when(step == 0)
    def _():
        dw_ref[...] = jnp.zeros_like(dw_ref)

    total = jnp.zeros((HEADS, 128), F32)
    for j in range(x_ref.shape[0]):
        hat, inv = normalize(x_ref[j])
        normed = (hat * gain).astype(BF16)
        db = tmp[:, j, :].astype(BF16)
        dx_ref[j] = normalize_grad(hat, inv, gain, tn(db, wt)).astype(BF16)
        total = total + nn(db, normed)
    dw_ref[...] += total


def pair_grad(pair, gain, wt, db):
    j, i, c = pair.shape
    step = 16
    return pl.pallas_call(
        pair_grad_kernel,
        grid=(j // step,),
        in_specs=[
            pl.BlockSpec((step, i, c), lambda g: (g, 0, 0)),
            pl.BlockSpec((1, c), lambda g: (0, 0)),
            pl.BlockSpec((HEADS, c), lambda g: (0, 0)),
            pl.BlockSpec((HEADS, step, i), lambda g: (0, g, 0)),
        ],
        out_specs=[
            pl.BlockSpec((step, i, c), lambda g: (g, 0, 0)),
            pl.BlockSpec((HEADS, c), lambda g: (0, 0)),
        ],
        out_shape=[
            jax.ShapeDtypeStruct((j, i, c), BF16),
            jax.ShapeDtypeStruct((HEADS, c), F32),
        ],
        scratch_shapes=[pltpu.VMEM((HEADS, step, i), F32)],
        compiler_params=params(),
        name="pair_grad",
    )(pair, gain, wt, db)


def swap(x, axis, groups=None):
    return lax.all_to_all(
        x, axis, split_axis=0, concat_axis=0, tiled=True, axis_index_groups=groups
    )


CORES = [[2 * m + c for m in range(8)] for c in range(2)]
OTHER = [(i, i ^ 1) for i in range(16)]


def gather_bias(x):
    core = lax.axis_index("seq") & 1
    mine = swap(jnp.broadcast_to(x[None], (8,) + x.shape), "seq", CORES)
    other = lax.ppermute(mine, "seq", OTHER)
    first = jnp.where(core == 0, mine, other)
    second = jnp.where(core == 0, other, mine)
    return jnp.stack([first, second], axis=1).reshape((16,) + x.shape)


def scatter_bias(x):
    core = lax.axis_index("seq") & 1
    x = x.reshape((8, 2) + x.shape[1:])
    send = lax.dynamic_index_in_dim(x, 1 - core, 1, keepdims=False)
    keep = lax.dynamic_index_in_dim(x, core, 1, keepdims=False)
    got = lax.ppermute(send, "seq", OTHER)
    both = (keep.astype(F32) + got.astype(F32)).astype(BF16)
    return jnp.sum(swap(both, "seq", CORES).astype(F32), axis=0).astype(BF16)


def local(x, gain, w, shift, wo, pair, pair_gain, wb, up):
    gain = gain.reshape(1, -1)
    shift = shift.reshape(1, -1)
    pair_gain = pair_gain.reshape(1, -1)
    wt = wb.T
    packed, gate, dg = project(x, gain, w, shift, wo, up)
    bias = pair_bias(pair, pair_gain, wt)
    bias = gather_bias(swap(bias, "res"))
    back, d_bias = attention(swap(packed, "res"), bias)
    d_bias = swap(scatter_bias(d_bias), "res")
    back = swap(back, "res")
    inc, dx, dw = finish(x, gain, w, wo, up, gate, dg, back)
    d_pair, dwb = pair_grad(pair, pair_gain, wt, d_bias)
    rows = jnp.concatenate(
        [dw.reshape(2560, 128), dwb.astype(BF16), jnp.zeros((120, 128), BF16)], axis=0
    ).reshape(128, 21, 128)
    part = jnp.sum(swap(rows, ("seq", "res")).astype(F32), axis=0).astype(BF16)
    rows = swap(jnp.broadcast_to(part[None], (128, 21, 128)), ("seq", "res"))
    rows = rows.reshape(2688, 128).astype(F32)
    dw = jnp.swapaxes(rows[:2560].reshape(10, 256, 128), 0, 1).reshape(256, 1280)
    return inc, dx, d_pair, dw[:, :1024], dw[:, 1024:], rows[2560:2568].T


def solution(mesh):
    tok = P("seq", "res", None)
    return jax.shard_map(
        local,
        mesh=mesh,
        in_specs=(tok, P(), P(), P(), P(), tok, P(), P(), tok),
        out_specs=(tok, tok, tok, P(), P(), P()),
        check_vma=False,
    )
```

```python
import functools

import jax
import jax.numpy as jnp
from jax import lax
from jax.experimental import pallas as pl
from jax.experimental.pallas import tpu as pltpu
from jax.sharding import PartitionSpec as P

EPS = 1e-05
F32 = jnp.float32
BF16 = jnp.bfloat16
HEADS = 8
DH = 32
SCALE = DH ** (-0.5)
VMEM = 48 * 1024 * 1024


def nn(a, b):
    return lax.dot_general(a, b, (((1,), (0,)), ((), ())), preferred_element_type=F32)


def nt(a, b):
    return lax.dot_general(a, b, (((1,), (1,)), ((), ())), preferred_element_type=F32)


def tn(a, b):
    return lax.dot_general(a, b, (((0,), (0,)), ((), ())), preferred_element_type=F32)


def normalize(x):
    x = x.astype(F32)
    centered = x - jnp.mean(x, axis=-1, keepdims=True)
    inv = lax.rsqrt(jnp.mean(centered * centered, axis=-1, keepdims=True) + EPS)
    return centered * inv, inv


def normalize_grad(hat, inv, gain, grad):
    g = grad * gain
    mean_g = jnp.mean(g, axis=-1, keepdims=True)
    mean_gx = jnp.mean(g * hat, axis=-1, keepdims=True)
    return inv * (g - mean_g - hat * mean_gx)


def cost(us):
    return pl.CostEstimate(flops=int(us * 1e9), bytes_accessed=int(us * 3e6), transcendentals=0)


def params(n=1):
    return pltpu.CompilerParams(
        dimension_semantics=("arbitrary",) * n, vmem_limit_bytes=VMEM
    )


def project_kernel(x_ref, gain_ref, w_ref, shift_ref, wo_ref, up_ref, pack_ref, gate_ref, dg_ref):
    hat, _ = normalize(x_ref[0])
    normed = (hat * gain_ref[...]).astype(BF16)
    proj = nn(normed, w_ref[...])
    q = (proj[:, :256] * SCALE).astype(BF16)
    k = proj[:, 256:512].astype(BF16)
    v = proj[:, 512:768].astype(BF16)
    gate = jax.nn.sigmoid(proj[:, 768:] + shift_ref[...])
    d_gated = nt(up_ref[0], wo_ref[...])
    da = (d_gated * gate).astype(BF16)
    gate_ref[0] = gate
    dg_ref[0] = d_gated
    for h in range(HEADS):
        c = slice(h * DH, (h + 1) * DH)
        pack_ref[h, 0] = jnp.concatenate([q[:, c], k[:, c], v[:, c], da[:, c]], axis=1)


def project(x, gain, w, shift, wo, up):
    s, n, c = x.shape
    whole = lambda *shape: pl.BlockSpec(shape, lambda i: (0,) * len(shape))
    row = pl.BlockSpec((1, n, c), lambda i: (i, 0, 0))
    return pl.pallas_call(
        project_kernel,
        grid=(s,),
        in_specs=[row, whole(1, c), whole(c, 4 * c), whole(1, c), whole(c, c), row],
        out_specs=[pl.BlockSpec((HEADS, 1, n, 128), lambda i: (0, i, 0, 0)), row, row],
        out_shape=[
            jax.ShapeDtypeStruct((HEADS, s, n, 128), BF16),
            jax.ShapeDtypeStruct((s, n, c), F32),
            jax.ShapeDtypeStruct((s, n, c), F32),
        ],
        compiler_params=params(),
        cost_estimate=cost(3),
        name="project",
    )(x, gain, w, shift, wo, up)


def bias_kernel(x_ref, gain_ref, wt_ref, out_ref, tmp):
    wt = wt_ref[...]
    for j in range(x_ref.shape[0]):
        hat, _ = normalize(x_ref[j])
        normed = (hat * gain_ref[...]).astype(BF16)
        tmp[:, j, :] = nt(wt, normed)
    out_ref[...] = tmp[...].astype(BF16)


def pair_bias(pair, gain, wt):
    j, i, c = pair.shape
    step = 16
    return pl.pallas_call(
        bias_kernel,
        grid=(j // step,),
        in_specs=[
            pl.BlockSpec((step, i, c), lambda g: (g, 0, 0)),
            pl.BlockSpec((1, c), lambda g: (0, 0)),
            pl.BlockSpec((HEADS, c), lambda g: (0, 0)),
        ],
        out_specs=pl.BlockSpec((HEADS, step, i), lambda g: (0, g, 0)),
        out_shape=jax.ShapeDtypeStruct((HEADS, j, i), BF16),
        scratch_shapes=[pltpu.VMEM((HEADS, step, i), F32)],
        compiler_params=params(),
        cost_estimate=cost(4),
        name="pair_bias",
    )(pair, gain, wt)


def attention_kernel(
    place_ref, x_ref, own_ref, other_ref, begin_ref, o_ref, down_ref, dother_ref,
    xr, xt, acc, scores, exps, dsc, rq, ra, delta, *, first, last,
):
    step = pl.program_id(0)
    n_seq = x_ref.shape[1]
    iw = 256
    core = place_ref[8]
    mine = pl.ds(pl.multiple_of(core * 64, 64), 64)
    others = pl.ds(pl.multiple_of((1 - core) * 64, 64), 64)
    zeros = lambda rows: jnp.zeros((rows, iw), BF16)

    @pl.when(step == 0)
    def _():
        for s in range(n_seq):
            for c in range(8):
                chip = place_ref[c]
                xr[c, s, 0:64] = x_ref[chip, s, mine]
                xr[c, s, 64:128] = x_ref[chip, s, others]
                xt[s, :, c * 128 : (c + 1) * 128] = xr[c, s].T
        acc[...] = jnp.zeros_like(acc) if begin_ref is None else begin_ref[...]

    ones = jnp.ones((16, 1024), BF16)
    for s in range(n_seq):
        block = 2 * step + first
        xq = jnp.concatenate([x_ref[block, s].T, x_ref[block + 1, s].T], axis=1)
        rhs_q = jnp.concatenate([zeros(32), xq[0:32], zeros(64)], axis=0)
        rq[s] = rhs_q
        top = jnp.full((8, iw), -jnp.inf, F32)
        for c in range(8):
            lo = jnp.concatenate([own_ref[c, 0], other_ref[c, 0]], axis=0)
            hi = jnp.concatenate([own_ref[c, 1], other_ref[c, 1]], axis=0)
            sc = nn(xr[c, s], rhs_q) + jnp.concatenate([lo, hi], axis=1).astype(F32)
            scores[c] = sc
            top = jnp.maximum(top, jnp.max(sc.reshape(16, 8, iw), axis=0))
        top = jnp.max(top, axis=0, keepdims=True)
        for c in range(8):
            exps[s, c] = jnp.exp(scores[c] - top).astype(BF16)
        left = jnp.concatenate([xt[s, 64:96, :], ones], axis=0)
        ot = nn(left, exps[s].reshape(1024, iw))
        inv = 1.0 / ot[32:33]
        ot = ot[0:32] * inv
        da = (xq[96:128].astype(F32) * inv).astype(BF16)
        delta[s] = jnp.sum(da.astype(F32) * ot, axis=0, keepdims=True)
        ra[s] = jnp.concatenate([zeros(64), da, zeros(32)], axis=0)
        for t in range(2):
            part = jnp.concatenate(
                [ot[:, t * 128 : (t + 1) * 128], jnp.zeros((96, 128), F32)], axis=0
            )
            acc[s, block + t] += part.T
    for c in range(8):
        total = jnp.zeros((128, iw), F32)
        chip = place_ref[c]
        for s in range(n_seq):
            e = exps[s, c]
            ds = e.astype(F32) * (nn(xr[c, s], ra[s]) - delta[s])
            total = total + ds
            ds = ds.astype(BF16)
            dsc[s, c] = ds
            more = nt(ds, rq[s]) + nt(e, ra[s])
            acc[s, chip, mine] += more[:64]
            acc[s, chip, others] += more[64:]
        low = total.astype(BF16)
        for t in range(2):
            down_ref[c, t] = low[:64, t * 128 : (t + 1) * 128]
            dother_ref[c, t] = low[64:, t * 128 : (t + 1) * 128]
    for s in range(n_seq):
        block = 2 * step + first
        dq = nn(xt[s, 32:64, :], dsc[s].reshape(1024, iw)) * SCALE
        for t in range(2):
            part = jnp.concatenate(
                [jnp.zeros((96, 128), F32), dq[:, t * 128 : (t + 1) * 128]], axis=0
            )
            acc[s, block + t] += part.T

    @pl.when(step == pl.num_programs(0) - 1)
    def _():
        if last:
            for s in range(n_seq):
                for r in range(8):
                    o_ref[r, s] = acc[s, r].astype(BF16)
        else:
            o_ref[...] = acc[...]


def attention(place, x, own, other, begin, first, last):
    r, s, n, _ = x.shape
    blocks = own.shape[1]
    half = pl.BlockSpec((8, 2, 64, 128), lambda g, p: (0, g, 0, 0))
    fixed = lambda *shape: pl.BlockSpec(shape, lambda g, p: (0, 0, 0, 0))
    body = functools.partial(attention_kernel, first=first, last=last)
    out = (r, s, n, 128) if last else (s, r, n, 128)
    if begin is None:
        kernel = lambda p, x, a, b, *rest: body(p, x, a, b, None, *rest)
        more, more_specs = (), []
    else:
        kernel, more, more_specs = body, (begin,), [fixed(s, r, n, 128)]
    return pl.pallas_call(
        kernel,
        grid_spec=pltpu.PrefetchScalarGridSpec(
            num_scalar_prefetch=1,
            grid=(blocks // 2,),
            in_specs=[fixed(r, s, n, 128), half, half] + more_specs,
            out_specs=[fixed(*out), half, half],
            scratch_shapes=[
                pltpu.VMEM((r, s, n, 128), BF16),
                pltpu.VMEM((s, 128, 1024), BF16),
                pltpu.VMEM((s, 8, 128, 128), F32),
                pltpu.VMEM((8, 128, 256), F32),
                pltpu.VMEM((s, 8, 128, 256), BF16),
                pltpu.VMEM((s, 8, 128, 256), BF16),
                pltpu.VMEM((s, 128, 256), BF16),
                pltpu.VMEM((s, 128, 256), BF16),
                pltpu.VMEM((s, 1, 256), F32),
            ],
        ),
        out_shape=[
            jax.ShapeDtypeStruct(out, BF16 if last else F32),
            jax.ShapeDtypeStruct((8, blocks, 64, 128), BF16),
            jax.ShapeDtypeStruct((8, blocks, 64, 128), BF16),
        ],
        compiler_params=params(),
        cost_estimate=cost(25),
        name="attention",
    )(place, x, own, other, *more)


def finish_kernel(
    x_ref, gain_ref, w_ref, wo_ref, up_ref, gate_ref, dg_ref, back_ref,
    inc_ref, dx_ref, dw_ref, acc,
):
    step = pl.program_id(0)
    hat, inv = normalize(x_ref[0])
    gain = gain_ref[...]
    normed = (hat * gain).astype(BF16)
    gate = gate_ref[0]
    d_gated = dg_ref[0]
    up = up_ref[0]
    back = [back_ref[h, 0] for h in range(HEADS)]
    pick = lambda a: jnp.concatenate([b[:, a * DH : (a + 1) * DH] for b in back], axis=1)
    attended = pick(0).astype(F32)
    gated = (gate * attended).astype(BF16)
    inc_ref[0] = nn(gated, wo_ref[...]).astype(BF16)
    d_pre = (d_gated * attended * gate * (1.0 - gate)).astype(BF16)
    d_proj = jnp.concatenate([pick(3), pick(1), pick(2), d_pre], axis=1)
    grad = nt(d_proj, w_ref[...])
    dx_ref[0] = normalize_grad(hat, inv, gain, grad).astype(BF16)

    @pl.when(step == 0)
    def _():
        acc[...] = jnp.zeros_like(acc)

    acc[:, :1024] += tn(normed, d_proj)
    acc[:, 1024:] += tn(gated, up)

    @pl.when(step == pl.num_programs(0) - 1)
    def _():
        for b in range(10):
            dw_ref[b] = acc[:, b * 128 : (b + 1) * 128].astype(BF16)


def finish(x, gain, w, wo, up, gate, dg, back):
    s, n, c = x.shape
    whole = lambda *shape: pl.BlockSpec(shape, lambda i: (0,) * len(shape))
    row = pl.BlockSpec((1, n, c), lambda i: (i, 0, 0))
    return pl.pallas_call(
        finish_kernel,
        grid=(s,),
        in_specs=[
            row, whole(1, c), whole(c, 4 * c), whole(c, c), row, row, row,
            pl.BlockSpec((HEADS, 1, n, 128), lambda i: (0, i, 0, 0)),
        ],
        out_specs=[row, row, whole(10, 256, 128)],
        out_shape=[
            jax.ShapeDtypeStruct((s, n, c), BF16),
            jax.ShapeDtypeStruct((s, n, c), BF16),
            jax.ShapeDtypeStruct((10, 256, 128), BF16),
        ],
        scratch_shapes=[pltpu.VMEM((c, 5 * c), F32)],
        compiler_params=params(),
        cost_estimate=cost(5),
        name="finish",
    )(x, gain, w, wo, up, gate, dg, back)


def pair_grad_kernel(x_ref, gain_ref, wt_ref, db_ref, dx_ref, dw_ref, tmp, spread):
    step = pl.program_id(0)
    gain = gain_ref[...]
    rows = x_ref.shape[0]
    tmp[...] = db_ref[...].astype(F32)

    @pl.when(step == 0)
    def _():
        dw_ref[...] = jnp.zeros_like(dw_ref)
        place = lax.broadcasted_iota(jnp.int32, (HEADS, rows, 128), 1)
        wide = jnp.broadcast_to(wt_ref[...].astype(F32)[:, None, :], (HEADS, rows, 128))
        for j in range(rows):
            block = jnp.where(place == j, wide, 0.0).reshape(HEADS * rows, 128)
            spread[:, j * 128 : (j + 1) * 128] = block.astype(BF16)

    turned = tmp[...].reshape(HEADS * rows, 128).T.astype(BF16)
    total = jnp.zeros((HEADS, 128), F32)
    for j in range(rows):
        hat, inv = normalize(x_ref[j])
        normed = (hat * gain).astype(BF16)
        grad = nn(turned, spread[:, j * 128 : (j + 1) * 128])
        dx_ref[j] = normalize_grad(hat, inv, gain, grad).astype(BF16)
        total = total + nn(tmp[:, j, :].astype(BF16), normed)
    dw_ref[...] += total


def pair_grad(pair, gain, wt, db):
    j, i, c = pair.shape
    step = 16
    return pl.pallas_call(
        pair_grad_kernel,
        grid=(j // step,),
        in_specs=[
            pl.BlockSpec((step, i, c), lambda g: (g, 0, 0)),
            pl.BlockSpec((1, c), lambda g: (0, 0)),
            pl.BlockSpec((HEADS, c), lambda g: (0, 0)),
            pl.BlockSpec((HEADS, step, i), lambda g: (0, g, 0)),
        ],
        out_specs=[
            pl.BlockSpec((step, i, c), lambda g: (g, 0, 0)),
            pl.BlockSpec((HEADS, c), lambda g: (0, 0)),
        ],
        out_shape=[
            jax.ShapeDtypeStruct((j, i, c), BF16),
            jax.ShapeDtypeStruct((HEADS, c), F32),
        ],
        scratch_shapes=[
            pltpu.VMEM((HEADS, step, i), F32),
            pltpu.VMEM((HEADS * step, step * 128), BF16),
        ],
        compiler_params=params(),
        cost_estimate=cost(5),
        name="pair_grad",
    )(pair, gain, wt, db)


def swap(x, axis):
    return lax.all_to_all(x, axis, split_axis=0, concat_axis=0, tiled=True)


OTHER = [(i, i ^ 1) for i in range(16)]
FAR = [(i, i ^ 8) for i in range(16)]


def along(shift):
    move = lambda i: (i & 9) | (((((i >> 1) & 3) + shift) % 4) << 1)
    return [(i, move(i)) for i in range(16)]


def send(x, pairs):
    return lax.ppermute(x, "seq", pairs)


def chip_order():
    me = lax.axis_index("seq")
    far, z, core = me >> 3, (me >> 1) & 3, me & 1
    chips = [(far ^ d) * 4 + ((z - shift) & 3) for shift in range(4) for d in range(2)]
    return jnp.stack(chips + [core]).astype(jnp.int32)


def device(far, low, z, x, core):
    return (far * 8 + z * 2 + core) * 8 + x * 2 + low


LAYERS = [
    [device(far, low, z, x, core) for z in range(4) for x in range(4)]
    for far in range(2)
    for low in range(2)
    for core in range(2)
]
ALL = ("seq", "res")


def layer_swap(x):
    return lax.all_to_all(
        x, ALL, split_axis=0, concat_axis=0, tiled=True, axis_index_groups=LAYERS
    )


def across(k):
    pairs = []
    for i in range(128):
        seq, res = divmod(i, 8)
        pairs.append((i, (seq ^ ((k >> 1) * 8)) * 8 + (res ^ (k & 1))))
    return pairs


def halve(rows):
    core = lax.axis_index("seq") & 1
    away = lax.dynamic_index_in_dim(rows, 1 - core, 0, keepdims=False)
    keep = lax.dynamic_index_in_dim(rows, core, 0, keepdims=False)
    return (keep.astype(F32) + send(away, OTHER).astype(F32)).astype(BF16)


def sum_layers(part, extra):
    part = jnp.sum(layer_swap(part).astype(F32), axis=0)
    part = jnp.concatenate([part, jnp.pad(extra, ((0, 8), (0, 0)))])
    low = part.astype(BF16)
    for k in (1, 2, 3):
        part = part + lax.ppermute(low, ALL, across(k)).astype(F32)
    part = part.astype(BF16)
    mine = layer_swap(jnp.broadcast_to(part[None], (16,) + part.shape))
    return mine, send(mine, OTHER)


def unpack_kernel(place_ref, mine_ref, other_ref, dw_ref, dwo_ref, dwb_ref):
    dwb_ref[...] = sum(
        ref[i, 80:96].astype(F32) for ref in (mine_ref, other_ref) for i in range(16)
    )[0:8]

    def write(low, high):
        get = lambda ref, b: jnp.concatenate(
            [ref[i, lo:hi].astype(F32) for i, lo, hi in block_rows(b)], axis=0
        )
        for b in range(10):
            block = get(low, b) if b < 5 else get(high, b - 5)
            if b < 8:
                dw_ref[:, b * 128 : (b + 1) * 128] = block
            else:
                dwo_ref[:, (b - 8) * 128 : (b - 7) * 128] = block

    @pl.when(place_ref[8] == 0)
    def _():
        write(mine_ref, other_ref)

    @pl.when(place_ref[8] != 0)
    def _():
        write(other_ref, mine_ref)


def block_rows(b):
    pieces = []
    row = b * 256
    while row < (b + 1) * 256:
        i, lo = divmod(row, 80)
        hi = min(80, lo + (b + 1) * 256 - row)
        pieces.append((i, lo, hi))
        row += hi - lo
    return pieces


def unpack(place, mine, other):
    fixed = lambda *shape: pl.BlockSpec(shape, lambda g, p: (0,) * len(shape))
    return pl.pallas_call(
        unpack_kernel,
        grid_spec=pltpu.PrefetchScalarGridSpec(
            num_scalar_prefetch=1,
            grid=(1,),
            in_specs=[fixed(16, 96, 128)] * 2,
            out_specs=[fixed(256, 1024), fixed(256, 256), fixed(8, 128)],
        ),
        out_shape=[
            jax.ShapeDtypeStruct((256, 1024), F32),
            jax.ShapeDtypeStruct((256, 256), F32),
            jax.ShapeDtypeStruct((8, 128), F32),
        ],
        compiler_params=params(),
        cost_estimate=cost(1),
        name="unpack",
    )(place, mine, other)


def local(x, gain, w, shift, wo, pair, pair_gain, wb, up):
    gain = gain.reshape(1, -1)
    shift = shift.reshape(1, -1)
    pair_gain = pair_gain.reshape(1, -1)
    wt = wb.T
    place = chip_order()
    bias = swap(pair_bias(pair, pair_gain, wt), "res")
    packed, gate, dg = project(x, gain, w, shift, wo, up)
    couple = jnp.stack([bias, send(bias, FAR)])
    couple, packed = lax.optimization_barrier((couple, packed))
    heads = swap(packed, "res")
    own = jnp.concatenate([couple] + [send(couple, along(shift)) for shift in (1, 2, 3)])
    own, heads = lax.optimization_barrier((own, heads))
    other = send(own, OTHER)
    back, d_own, d_other = attention(place, heads, own, other, None, 0, True)
    back = swap(back, "res")
    both = d_own.astype(F32) + send(d_other, OTHER).astype(F32)
    low = both.astype(BF16)
    total = both[0:2]
    for turn in (1, 2, 3):
        total = total + send(low[2 * turn : 2 * turn + 2], along(-turn)).astype(F32)
    keep, away = total[0], total[1].astype(BF16)
    keep, away, back = lax.optimization_barrier((keep, away, back))
    d_bias = (keep + send(away, FAR).astype(F32)).astype(BF16)
    d_bias = swap(d_bias, "res")
    inc, dx, dw = finish(x, gain, w, wo, up, gate, dg, back)
    part = halve(dw.reshape(2, 16, 80, 128))
    d_bias, part = lax.optimization_barrier((d_bias, part))
    d_pair, dwb = pair_grad(pair, pair_gain, wt, d_bias)
    dw, dwo, dwb = unpack(place, *sum_layers(part, dwb))
    return inc, dx, d_pair, dw, dwo, dwb.T


def solution(mesh):
    tok = P("seq", "res", None)
    return jax.shard_map(
        local,
        mesh=mesh,
        in_specs=(tok, P(), P(), P(), P(), tok, P(), P(), tok),
        out_specs=(tok, tok, tok, P(), P(), P()),
        check_vma=False,
    )
```

```python
import functools

import jax
import jax.numpy as jnp
from jax import lax
from jax.experimental import pallas as pl
from jax.experimental.pallas import tpu as pltpu
from jax.sharding import PartitionSpec as P

EPS = 1e-05
F32 = jnp.float32
BF16 = jnp.bfloat16
HEADS = 8
DH = 32
SCALE = DH ** (-0.5)


def nn(a, b):
    return lax.dot_general(a, b, (((1,), (0,)), ((), ())), preferred_element_type=F32)


def nt(a, b):
    return lax.dot_general(a, b, (((1,), (1,)), ((), ())), preferred_element_type=F32)


def tn(a, b):
    return lax.dot_general(a, b, (((0,), (0,)), ((), ())), preferred_element_type=F32)


def normalize(x):
    x = x.astype(F32)
    centered = x - jnp.mean(x, axis=-1, keepdims=True)
    inv = lax.rsqrt(jnp.mean(centered * centered, axis=-1, keepdims=True) + EPS)
    return centered * inv, inv


def normalize_grad(hat, inv, gain, grad):
    g = grad * gain
    mean_g = jnp.mean(g, axis=-1, keepdims=True)
    mean_gx = jnp.mean(g * hat, axis=-1, keepdims=True)
    return inv * (g - mean_g - hat * mean_gx)


def split(x):
    high = x.astype(BF16)
    return jnp.concatenate([high, (x - high.astype(F32)).astype(BF16)], axis=1)


def row_mean(x, ones):
    return nn(split(x), ones)


def normalize_pairs(x, ones):
    centered = x.astype(F32) - nn(x, ones[:128])
    inv = lax.rsqrt(row_mean(centered * centered, ones) + EPS)
    return centered * inv, inv


def cost(us):
    return pl.CostEstimate(flops=int(us * 1e9), bytes_accessed=int(us * 3e6), transcendentals=0)


def params(megabytes=60):
    return pltpu.CompilerParams(
        dimension_semantics=("arbitrary",), vmem_limit_bytes=megabytes * 1024 * 1024
    )


def project_kernel(x_ref, gain_ref, w_ref, shift_ref, wo_ref, up_ref, pack_ref, gate_ref, dg_ref):
    seqs, rows, width = x_ref.shape
    flat = lambda ref: ref[...].reshape(seqs * rows, width)
    hat, _ = normalize(flat(x_ref))
    normed = (hat * gain_ref[...]).astype(BF16)
    proj = nn(normed, w_ref[...])
    q = (proj[:, :256] * SCALE).astype(BF16)
    k = proj[:, 256:512].astype(BF16)
    v = proj[:, 512:768].astype(BF16)
    gate = jax.nn.sigmoid(proj[:, 768:] + shift_ref[...])
    d_gated = nt(flat(up_ref), wo_ref[...])
    da = (d_gated * gate).astype(BF16)
    gate_ref[...] = gate.reshape(seqs, rows, width)
    dg_ref[...] = d_gated.reshape(seqs, rows, width)
    for h in range(HEADS):
        c = slice(h * DH, (h + 1) * DH)
        packed = jnp.concatenate([q[:, c], k[:, c], v[:, c], da[:, c]], axis=1)
        pack_ref[h] = packed.reshape(seqs, rows, 128)


def project(x, gain, w, shift, wo, up):
    s, n, c = x.shape
    whole = lambda *shape: pl.BlockSpec(shape, lambda i: (0,) * len(shape))
    row = pl.BlockSpec((2, n, c), lambda i: (i, 0, 0))
    return pl.pallas_call(
        project_kernel,
        grid=(s // 2,),
        in_specs=[row, whole(1, c), whole(c, 4 * c), whole(1, c), whole(c, c), row],
        out_specs=[pl.BlockSpec((HEADS, 2, n, 128), lambda i: (0, i, 0, 0)), row, row],
        out_shape=[
            jax.ShapeDtypeStruct((HEADS, s, n, 128), BF16),
            jax.ShapeDtypeStruct((s, n, c), F32),
            jax.ShapeDtypeStruct((s, n, c), F32),
        ],
        compiler_params=params(),
        cost_estimate=cost(3),
        name="project",
    )(x, gain, w, shift, wo, up)


def bias_kernel(x_ref, gain_ref, wt_ref, out_ref, normed_ref, tmp):
    ones = jnp.full((256, 128), 1 / 128, BF16)
    rows = x_ref.shape[0]
    hat, _ = normalize_pairs(x_ref[...].reshape(rows * 128, 128), ones)
    normed = (hat * gain_ref[...]).astype(BF16).reshape(rows, 128, 128)
    normed_ref[...] = normed
    flat = nt(wt_ref[...], normed.reshape(rows * 128, 128))
    for j in range(rows):
        tmp[:, j, :] = flat[:, j * 128 : (j + 1) * 128]
    low = tmp[...].astype(BF16)
    out_ref[0] = low
    out_ref[1] = low


def pair_bias(pair, gain, wt):
    j, i, c = pair.shape
    step = 32
    return pl.pallas_call(
        bias_kernel,
        grid=(j // step,),
        in_specs=[
            pl.BlockSpec((step, i, c), lambda g: (g, 0, 0)),
            pl.BlockSpec((1, c), lambda g: (0, 0)),
            pl.BlockSpec((HEADS, c), lambda g: (0, 0)),
        ],
        out_specs=[
            pl.BlockSpec((2, HEADS, step, i), lambda g: (0, 0, g, 0)),
            pl.BlockSpec((step, i, c), lambda g: (g, 0, 0)),
        ],
        out_shape=[
            jax.ShapeDtypeStruct((2, HEADS, j, i), BF16),
            jax.ShapeDtypeStruct((j, i, c), BF16),
        ],
        scratch_shapes=[pltpu.VMEM((HEADS, step, i), F32)],
        compiler_params=params(),
        cost_estimate=cost(4),
        name="pair_bias",
    )(pair, gain, wt)


def attention_kernel(
    place_ref, x_ref, own_ref, other_ref, o_ref, down_ref, dother_ref,
    xr, xt, acc, qd, scores, ed, total,
):
    step = pl.program_id(0)
    n_seq = x_ref.shape[1]
    iw = 256
    core = place_ref[8]
    mine = pl.ds(pl.multiple_of(core * 64, 64), 64)
    others = pl.ds(pl.multiple_of((1 - core) * 64, 64), 64)
    zeros = lambda rows: jnp.zeros((rows, iw), BF16)

    @pl.when(step == 0)
    def _():
        for s in range(n_seq):
            for c in range(8):
                chip = place_ref[c]
                xr[c, s, 0:64] = x_ref[chip, s, mine]
                xr[c, s, 64:128] = x_ref[chip, s, others]
                xt[s, :, c * 128 : (c + 1) * 128] = xr[c, s].T
        acc[...] = jnp.zeros_like(acc)

    ones = jnp.ones((16, 1024), BF16)
    block = 2 * step

    def score(s):
        xq = jnp.concatenate([x_ref[block, s].T, x_ref[block + 1, s].T], axis=1)
        rhs_q = jnp.concatenate([zeros(32), xq[0:32], zeros(64)], axis=0)
        top = jnp.full((8, iw), -jnp.inf, F32)
        k = 8
        for d in range(0, 8, k):
            big = nn(xr[d : d + k, s].reshape(k * 128, 128), rhs_q)
            for c in range(d, d + k):
                lo = jnp.concatenate([own_ref[c, 0], other_ref[c, 0]], axis=0)
                hi = jnp.concatenate([own_ref[c, 1], other_ref[c, 1]], axis=0)
                sc = big[(c - d) * 128 : (c - d + 1) * 128]
                sc = sc + jnp.concatenate([lo, hi], axis=1).astype(F32)
                scores[s % 2, c] = sc
                top = jnp.maximum(top, jnp.max(sc.reshape(16, 8, iw), axis=0))
                yield
        return xq, rhs_q, jnp.max(top, axis=0, keepdims=True)

    def weigh(s, xq, top):
        for c in range(8):
            ed[s % 2, c, :, :iw] = jnp.exp(scores[s % 2, c] - top).astype(BF16)
            yield
        left = jnp.concatenate([xt[s, 64:96, :], ones], axis=0)
        ot = nn(left, ed[s % 2, :, :, :iw].reshape(1024, iw))
        inv = 1.0 / ot[32:33]
        ot = ot[0:32] * inv
        da = (xq[96:128].astype(F32) * inv).astype(BF16)
        delta = jnp.sum(da.astype(F32) * ot, axis=0, keepdims=True)
        rhs_a = jnp.concatenate([zeros(64), da, zeros(32)], axis=0)
        return ot, rhs_a, delta

    def back(s, rhs_q, rhs_a, delta, ot):
        k = 8
        for c in range(8):
            if c % k == 0:
                big = nn(xr[c : c + k, s].reshape(k * 128, 128), rhs_a)
            e = ed[s % 2, c, :, :iw]
            ds = e.astype(F32) * (big[c % k * 128 : (c % k + 1) * 128] - delta)
            low = ds.astype(BF16)
            ed[s % 2, c, :, iw:] = low
            if s == 0:
                total[c] = ds
            elif s < n_seq - 1:
                total[c] += ds
            else:
                low = (total[c] + ds).astype(BF16)
                for t in range(2):
                    down_ref[c, t] = low[:64, t * 128 : (t + 1) * 128]
                    dother_ref[c, t] = low[64:, t * 128 : (t + 1) * 128]
            if (c + 1) % 8 == 0:
                w = slice(c + 1 - 8, c + 1)
                both = jnp.concatenate([rhs_a, rhs_q], axis=1)
                more = nt(ed[s % 2, w].reshape(8 * 128, 2 * iw), both)
                acc[s, w] += more.reshape(8, 128, 128)
            yield
        dq = nn(xt[s, 32:64, :], ed[s % 2, :, :, iw:].reshape(1024, iw)) * SCALE
        both = jnp.concatenate([ot, jnp.zeros((64, iw), F32), dq], axis=0)
        for t in range(2):
            qd[s, block + t] = both[:, t * 128 : (t + 1) * 128].T

    state = {}

    def drive(gens):
        live = list(gens)
        while live:
            for item in list(live):
                key, gen = item
                try:
                    next(gen)
                except StopIteration as stop:
                    state[key] = stop.value
                    live.remove(item)

    for t in range(n_seq + 2):
        gens = []
        if 0 <= t - 2 < n_seq:
            s = t - 2
            xq, rhs_q, top = state["s", s]
            ot, rhs_a, delta = state["w", s]
            late = (("b", s), back(s, rhs_q, rhs_a, delta, ot))
        if 0 <= t - 1 < n_seq:
            s = t - 1
            xq, rhs_q, top = state["s", s]
            gens.append((("w", s), weigh(s, xq, top)))
        if t < n_seq:
            gens.append((("s", t), score(t)))
        if t >= 2:
            gens.append(late)
        drive(gens)

    @pl.when(step == pl.num_programs(0) - 1)
    def _():
        for s in range(n_seq):
            for c in range(8):
                chip = place_ref[c]
                o_ref[chip, s, mine] = (acc[s, c, 0:64] + qd[s, chip, mine]).astype(BF16)
                o_ref[chip, s, others] = (acc[s, c, 64:128] + qd[s, chip, others]).astype(BF16)


def attention(place, x, own, other):
    r, s, n, _ = x.shape
    half = pl.BlockSpec((8, 2, 64, 128), lambda g, p: (0, g, 0, 0))
    whole = pl.BlockSpec((r, s, n, 128), lambda g, p: (0, 0, 0, 0))
    return pl.pallas_call(
        attention_kernel,
        grid_spec=pltpu.PrefetchScalarGridSpec(
            num_scalar_prefetch=1,
            grid=(4,),
            in_specs=[whole, half, half],
            out_specs=[whole, half, half],
            scratch_shapes=[
                pltpu.VMEM((r, s, n, 128), BF16),
                pltpu.VMEM((s, 128, 1024), BF16),
                pltpu.VMEM((s, 8, 128, 128), F32),
                pltpu.VMEM((s, 8, 128, 128), F32),
                pltpu.VMEM((2, 8, 128, 256), F32),
                pltpu.VMEM((2, 8, 128, 512), BF16),
                pltpu.VMEM((8, 128, 256), F32),
            ],
        ),
        out_shape=[
            jax.ShapeDtypeStruct((r, s, n, 128), BF16),
            jax.ShapeDtypeStruct((8, r, 64, 128), BF16),
            jax.ShapeDtypeStruct((8, r, 64, 128), BF16),
        ],
        compiler_params=params(),
        cost_estimate=cost(18),
        name="attention",
    )(place, x, own, other)


def finish_kernel(
    place_ref, x_ref, gain_ref, w_ref, wo_ref, up_ref, gate_ref, dg_ref, back_ref,
    inc_ref, dx_ref, keep_ref, away_ref, acc,
):
    step = pl.program_id(0)
    seqs, rows, width = x_ref.shape
    flat = lambda ref: ref[...].reshape(seqs * rows, width)
    hat, inv = normalize(flat(x_ref))
    gain = gain_ref[...]
    normed = (hat * gain).astype(BF16)
    gate = flat(gate_ref)
    d_gated = flat(dg_ref)
    up = flat(up_ref)
    back = [back_ref[h].reshape(seqs * rows, 128) for h in range(HEADS)]
    pick = lambda a: jnp.concatenate([b[:, a * DH : (a + 1) * DH] for b in back], axis=1)
    attended = pick(0).astype(F32)
    gated = (gate * attended).astype(BF16)
    inc_ref[...] = nn(gated, wo_ref[...]).astype(BF16).reshape(seqs, rows, width)
    d_pre = (d_gated * attended * gate * (1.0 - gate)).astype(BF16)
    d_proj = jnp.concatenate([pick(3), pick(1), pick(2), d_pre], axis=1)
    grad = nt(d_proj, w_ref[...])
    grad = normalize_grad(hat, inv, gain, grad).astype(BF16)
    dx_ref[...] = grad.reshape(seqs, rows, width)

    @pl.when(step == 0)
    def _():
        acc[...] = jnp.zeros_like(acc)

    acc[:, :1024] += tn(normed, d_proj)
    acc[:, 1024:] += tn(gated, up)

    last = step == pl.num_programs(0) - 1
    core = place_ref[8]

    def write(low_ref, high_ref):
        for b in range(5):
            low_ref[b] = acc[:, b * 128 : (b + 1) * 128].astype(BF16)
            high_ref[b] = acc[:, (b + 5) * 128 : (b + 6) * 128].astype(BF16)

    @pl.when(jnp.logical_and(last, core == 0))
    def _():
        write(keep_ref, away_ref)

    @pl.when(jnp.logical_and(last, core != 0))
    def _():
        write(away_ref, keep_ref)


def finish(place, x, gain, w, wo, up, gate, dg, back):
    s, n, c = x.shape
    whole = lambda *shape: pl.BlockSpec(shape, lambda i, p: (0,) * len(shape))
    row = pl.BlockSpec((2, n, c), lambda i, p: (i, 0, 0))
    return pl.pallas_call(
        finish_kernel,
        grid_spec=pltpu.PrefetchScalarGridSpec(
            num_scalar_prefetch=1,
            grid=(s // 2,),
            in_specs=[
                row, whole(1, c), whole(c, 4 * c), whole(c, c), row, row, row,
                pl.BlockSpec((HEADS, 2, n, 128), lambda i, p: (0, i, 0, 0)),
            ],
            out_specs=[row, row, whole(5, 256, 128), whole(5, 256, 128)],
            scratch_shapes=[pltpu.VMEM((c, 5 * c), F32)],
        ),
        out_shape=[
            jax.ShapeDtypeStruct((s, n, c), BF16),
            jax.ShapeDtypeStruct((s, n, c), BF16),
            jax.ShapeDtypeStruct((5, 256, 128), BF16),
            jax.ShapeDtypeStruct((5, 256, 128), BF16),
        ],
        compiler_params=params(),
        cost_estimate=cost(5),
        name="finish",
    )(place, x, gain, w, wo, up, gate, dg, back)


def pair_weight_kernel(n_ref, db_ref, dw_ref, tmp):
    tmp[...] = db_ref[0].astype(F32) + db_ref[1].astype(F32)
    total = jnp.zeros((HEADS, 128), F32)
    for j in range(n_ref.shape[0]):
        total = total + nn(tmp[:, j, :].astype(BF16), n_ref[j])

    @pl.when(pl.program_id(0) == 0)
    def _():
        dw_ref[...] = total

    @pl.when(pl.program_id(0) > 0)
    def _():
        dw_ref[...] += total


def pair_weight(normed, db):
    j, i, c = normed.shape
    step = 32
    return pl.pallas_call(
        pair_weight_kernel,
        grid=(j // step,),
        in_specs=[
            pl.BlockSpec((step, i, c), lambda g: (g, 0, 0)),
            pl.BlockSpec((2, HEADS, step, i), lambda g: (0, 0, g, 0)),
        ],
        out_specs=pl.BlockSpec((HEADS, c), lambda g: (0, 0)),
        out_shape=jax.ShapeDtypeStruct((HEADS, c), F32),
        scratch_shapes=[pltpu.VMEM((HEADS, step, i), F32)],
        compiler_params=params(),
        cost_estimate=cost(2),
        name="pair_weight",
    )(normed, db)


def pair_grad_kernel(x_ref, gain_ref, wt_ref, db_ref, dx_ref, spread):
    step = pl.program_id(0)
    gain = gain_ref[...]
    rows = x_ref.shape[0]
    ones = jnp.full((256, 128), 1 / 128, BF16)

    @pl.when(step == 0)
    def _():
        place = lax.broadcasted_iota(jnp.int32, (HEADS, rows, 128), 1)
        weight = wt_ref[...].astype(F32) * gain
        mean = jnp.broadcast_to(jnp.mean(weight, axis=1, keepdims=True), (HEADS, 128))
        parts = []
        for value in (weight, mean):
            high = value.astype(BF16).astype(F32)
            parts.append((high, value - high))
        for j in range(rows):
            for t in range(2):
                for k in range(2):
                    wide = jnp.broadcast_to(parts[t][k][:, None, :], (HEADS, rows, 128))
                    block = jnp.where(place == j, wide, 0.0).reshape(HEADS * rows, 128)
                    spread[j, k * 128 : (k + 1) * 128, t * 128 : (t + 1) * 128] = block.astype(
                        BF16
                    )

    db = db_ref[0].astype(F32) + db_ref[1].astype(F32)
    turned = db.reshape(HEADS * rows, 128).T.astype(BF16)
    turned = jnp.concatenate([turned, turned], axis=1)
    hat, inv = normalize_pairs(x_ref[...].reshape(rows * 128, 128), ones)
    both = [nn(turned, spread[j]) for j in range(rows)]
    grad = jnp.concatenate([b[:, :128] for b in both], axis=0)
    mean = jnp.concatenate([b[:, 128:] for b in both], axis=0)
    out = inv * (grad - mean - hat * row_mean(grad * hat, ones))
    dx_ref[...] = out.astype(BF16).reshape(rows, 128, 128)


def pair_grad(pair, gain, wt, db):
    j, i, c = pair.shape
    step = 16
    return pl.pallas_call(
        pair_grad_kernel,
        grid=(j // step,),
        in_specs=[
            pl.BlockSpec((step, i, c), lambda g: (g, 0, 0)),
            pl.BlockSpec((1, c), lambda g: (0, 0)),
            pl.BlockSpec((HEADS, c), lambda g: (0, 0)),
            pl.BlockSpec((2, HEADS, step, i), lambda g: (0, 0, g, 0)),
        ],
        out_specs=pl.BlockSpec((step, i, c), lambda g: (g, 0, 0)),
        out_shape=jax.ShapeDtypeStruct((j, i, c), BF16),
        scratch_shapes=[pltpu.VMEM((step, 2 * HEADS * step, 256), BF16)],
        compiler_params=params(),
        cost_estimate=cost(8),
        name="pair_grad",
    )(pair, gain, wt, db)


def swap(x, axis):
    return lax.all_to_all(x, axis, split_axis=0, concat_axis=0, tiled=True)


OTHER = [(i, i ^ 1) for i in range(16)]


def along(shift):
    move = lambda i: (i & 9) | (((((i >> 1) & 3) + shift) % 4) << 1)
    return [(i, move(i)) for i in range(16)]


def send(x, pairs):
    return lax.ppermute(x, "seq", pairs)


def chip_order():
    me = lax.axis_index("seq")
    z, core = (me >> 1) & 3, me & 1
    chips = [d * 4 + ((z - shift) & 3) for shift in range(4) for d in range(2)]
    return jnp.stack(chips + [core]).astype(jnp.int32)


def device(far, low, z, x, core):
    return (far * 8 + z * 2 + core) * 8 + x * 2 + low


LAYERS = [
    [device(far, low, z, x, core) for z in range(4) for x in range(4)]
    for far in range(2)
    for low in range(2)
    for core in range(2)
]
ALL = ("seq", "res")


COLUMNS = [
    [(far * 8 + line) * 8 + res for far in range(2) for res in range(8)] for line in range(8)
]


def group_swap(x, groups):
    return lax.all_to_all(
        x, ALL, split_axis=0, concat_axis=0, tiled=True, axis_index_groups=groups
    )


def across(k):
    pairs = []
    for i in range(128):
        seq, res = divmod(i, 8)
        pairs.append((i, (seq ^ ((k >> 1) * 8)) * 8 + (res ^ (k & 1))))
    return pairs


def sum_layers(part, extra):
    part = jnp.sum(group_swap(part, LAYERS).astype(F32), axis=0)
    part = jnp.concatenate([part, jnp.pad(extra, ((0, 8), (0, 0)))])
    low = part.astype(BF16)
    for k in (1, 2, 3):
        part = part + lax.ppermute(low, ALL, across(k)).astype(F32)
    part = part.astype(BF16)
    return group_swap(jnp.broadcast_to(part[None], (16,) + part.shape), LAYERS)


def unpack_kernel(place_ref, mine_ref, other_ref, dw_ref, dwo_ref, dwb_ref):
    dwb_ref[...] = sum(
        ref[i, 80:96].astype(F32) for ref in (mine_ref, other_ref) for i in range(16)
    )[0:8]

    def write(low, high):
        get = lambda ref, b: jnp.concatenate(
            [ref[i, lo:hi].astype(F32) for i, lo, hi in block_rows(b)], axis=0
        )
        for b in range(10):
            block = get(low, b) if b < 5 else get(high, b - 5)
            if b < 8:
                dw_ref[:, b * 128 : (b + 1) * 128] = block
            else:
                dwo_ref[:, (b - 8) * 128 : (b - 7) * 128] = block

    @pl.when(place_ref[8] == 0)
    def _():
        write(mine_ref, other_ref)

    @pl.when(place_ref[8] != 0)
    def _():
        write(other_ref, mine_ref)


def block_rows(b):
    pieces = []
    row = b * 256
    while row < (b + 1) * 256:
        i, lo = divmod(row, 80)
        hi = min(80, lo + (b + 1) * 256 - row)
        pieces.append((i, lo, hi))
        row += hi - lo
    return pieces


def unpack(place, mine, other):
    fixed = lambda *shape: pl.BlockSpec(shape, lambda g, p: (0,) * len(shape))
    return pl.pallas_call(
        unpack_kernel,
        grid_spec=pltpu.PrefetchScalarGridSpec(
            num_scalar_prefetch=1,
            grid=(1,),
            in_specs=[fixed(16, 96, 128)] * 2,
            out_specs=[fixed(256, 1024), fixed(256, 256), fixed(8, 128)],
        ),
        out_shape=[
            jax.ShapeDtypeStruct((256, 1024), F32),
            jax.ShapeDtypeStruct((256, 256), F32),
            jax.ShapeDtypeStruct((8, 128), F32),
        ],
        compiler_params=params(16),
        cost_estimate=cost(1),
        name="unpack",
    )(place, mine, other)


def local(x, gain, w, shift, wo, pair, pair_gain, wb, up):
    gain = gain.reshape(1, -1)
    shift = shift.reshape(1, -1)
    pair_gain = pair_gain.reshape(1, -1)
    wt = wb.T
    place = chip_order()
    bias, normed = pair_bias(pair, pair_gain, wt)
    couple = group_swap(bias.reshape(16, 64, 128), COLUMNS).reshape(2, 8, 64, 128)
    packed, gate, dg = project(x, gain, w, shift, wo, up)
    couple, packed = lax.optimization_barrier((couple, packed))
    heads = swap(packed, "res")
    own = jnp.concatenate([couple] + [send(couple, along(turn)) for turn in (1, 2, 3)])
    own, heads = lax.optimization_barrier((own, heads))
    other = send(own, OTHER)
    back, d_own, d_other = attention(place, heads, own, other)
    back = swap(back, "res")
    low = (d_own.astype(F32) + send(d_other, OTHER).astype(F32)).astype(BF16)
    total = low[0:2].astype(F32)
    for turn in (1, 2, 3):
        total = total + send(low[2 * turn : 2 * turn + 2], along(-turn)).astype(F32)
    d_bias = group_swap(total.astype(BF16).reshape(16, 64, 128), COLUMNS).reshape(2, 8, 64, 128)
    inc, dx, keep, away = finish(place, x, gain, w, wo, up, gate, dg, back)
    d_bias, away = lax.optimization_barrier((d_bias, away))
    part = (keep.astype(F32) + send(away, OTHER).astype(F32)).astype(BF16)
    part = part.reshape(16, 80, 128)
    dwb = pair_weight(normed, d_bias)
    mine = sum_layers(part, dwb)
    d_pair = pair_grad(pair, pair_gain, wt, d_bias)
    mine, d_pair = lax.optimization_barrier((mine, d_pair))
    dw, dwo, dwb = unpack(place, mine, send(mine, OTHER))
    return inc, dx, d_pair, dw, dwo, dwb.T


def solution(mesh):
    tok = P("seq", "res", None)
    return jax.shard_map(
        local,
        mesh=mesh,
        in_specs=(tok, P(), P(), P(), P(), tok, P(), P(), tok),
        out_specs=(tok, tok, tok, P(), P(), P()),
        check_vma=False,
    )
```

```python
import functools

import jax
import jax.numpy as jnp
from jax import lax
from jax.experimental import pallas as pl
from jax.experimental.pallas import tpu as pltpu
from jax.sharding import PartitionSpec as P

EPS = 1e-05
F32 = jnp.float32
BF16 = jnp.bfloat16
HEADS = 8
DH = 32
SCALE = DH ** (-0.5)


def nn(a, b):
    return lax.dot_general(a, b, (((1,), (0,)), ((), ())), preferred_element_type=F32)


def nt(a, b):
    return lax.dot_general(a, b, (((1,), (1,)), ((), ())), preferred_element_type=F32)


def tn(a, b):
    return lax.dot_general(a, b, (((0,), (0,)), ((), ())), preferred_element_type=F32)


def normalize(x):
    x = x.astype(F32)
    centered = x - jnp.mean(x, axis=-1, keepdims=True)
    inv = lax.rsqrt(jnp.mean(centered * centered, axis=-1, keepdims=True) + EPS)
    return centered * inv, inv


def normalize_grad(hat, inv, gain, grad):
    g = grad * gain
    mean_g = jnp.mean(g, axis=-1, keepdims=True)
    mean_gx = jnp.mean(g * hat, axis=-1, keepdims=True)
    return inv * (g - mean_g - hat * mean_gx)


def row_mean(x, ones):
    return nn(x.astype(BF16), ones)


def normalize_pairs(x, ones):
    centered = x.astype(F32) - nn(x, ones)
    inv = lax.rsqrt(row_mean(centered * centered, ones) + EPS)
    return centered * inv, inv


def cost(us):
    return pl.CostEstimate(flops=int(us * 1e9), bytes_accessed=int(us * 3e6), transcendentals=0)


def params(megabytes=60):
    return pltpu.CompilerParams(
        dimension_semantics=("arbitrary",), vmem_limit_bytes=megabytes * 1024 * 1024
    )


def project_kernel(x_ref, gain_ref, w_ref, shift_ref, wo_ref, up_ref, pack_ref, gate_ref, dg_ref):
    seqs, rows, width = x_ref.shape
    flat = lambda ref: ref[...].reshape(seqs * rows, width)
    hat, _ = normalize(flat(x_ref))
    normed = (hat * gain_ref[...]).astype(BF16)
    proj = nn(normed, w_ref[...])
    q = (proj[:, :256] * SCALE).astype(BF16)
    k = proj[:, 256:512].astype(BF16)
    v = proj[:, 512:768].astype(BF16)
    gate = jax.nn.sigmoid(proj[:, 768:] + shift_ref[...])
    d_gated = nt(flat(up_ref), wo_ref[...])
    da = (d_gated * gate).astype(BF16)
    gate_ref[...] = gate.reshape(seqs, rows, width)
    dg_ref[...] = d_gated.reshape(seqs, rows, width)
    for h in range(HEADS):
        c = slice(h * DH, (h + 1) * DH)
        packed = jnp.concatenate([q[:, c], k[:, c], v[:, c], da[:, c]], axis=1)
        pack_ref[h] = packed.reshape(seqs, rows, 128)


def project(x, gain, w, shift, wo, up):
    s, n, c = x.shape
    whole = lambda *shape: pl.BlockSpec(shape, lambda i: (0,) * len(shape))
    row = pl.BlockSpec((2, n, c), lambda i: (i, 0, 0))
    return pl.pallas_call(
        project_kernel,
        grid=(s // 2,),
        in_specs=[row, whole(1, c), whole(c, 4 * c), whole(1, c), whole(c, c), row],
        out_specs=[pl.BlockSpec((HEADS, 2, n, 128), lambda i: (0, i, 0, 0)), row, row],
        out_shape=[
            jax.ShapeDtypeStruct((HEADS, s, n, 128), BF16),
            jax.ShapeDtypeStruct((s, n, c), F32),
            jax.ShapeDtypeStruct((s, n, c), F32),
        ],
        compiler_params=params(),
        cost_estimate=cost(3),
        name="project",
    )(x, gain, w, shift, wo, up)


def bias_kernel(x_ref, gain_ref, wt_ref, out_ref, normed_ref, tmp):
    ones = jnp.full((128, 128), 1 / 128, BF16)
    rows = x_ref.shape[0]
    hat, _ = normalize_pairs(x_ref[...].reshape(rows * 128, 128), ones)
    normed = (hat * gain_ref[...]).astype(BF16).reshape(rows, 128, 128)
    normed_ref[...] = normed
    flat = nt(wt_ref[...], normed.reshape(rows * 128, 128))
    for j in range(rows):
        tmp[:, j, :] = flat[:, j * 128 : (j + 1) * 128]
    low = tmp[...].astype(BF16)
    out_ref[0] = low
    out_ref[1] = low


def pair_bias(pair, gain, wt):
    j, i, c = pair.shape
    step = 32
    return pl.pallas_call(
        bias_kernel,
        grid=(j // step,),
        in_specs=[
            pl.BlockSpec((step, i, c), lambda g: (g, 0, 0)),
            pl.BlockSpec((1, c), lambda g: (0, 0)),
            pl.BlockSpec((HEADS, c), lambda g: (0, 0)),
        ],
        out_specs=[
            pl.BlockSpec((2, HEADS, step, i), lambda g: (0, 0, g, 0)),
            pl.BlockSpec((step, i, c), lambda g: (g, 0, 0)),
        ],
        out_shape=[
            jax.ShapeDtypeStruct((2, HEADS, j, i), BF16),
            jax.ShapeDtypeStruct((j, i, c), BF16),
        ],
        scratch_shapes=[pltpu.VMEM((HEADS, step, i), F32)],
        compiler_params=params(),
        cost_estimate=cost(4),
        name="pair_bias",
    )(pair, gain, wt)


def attention_kernel(
    place_ref, x_ref, own_ref, other_ref, o_ref, down_ref, dother_ref,
    xr, xt, acc, qd, scores, ed, total,
):
    step = pl.program_id(0)
    n_seq = x_ref.shape[1]
    iw = 256
    core = place_ref[8]
    mine = pl.ds(pl.multiple_of(core * 64, 64), 64)
    others = pl.ds(pl.multiple_of((1 - core) * 64, 64), 64)
    zeros = lambda rows: jnp.zeros((rows, iw), BF16)

    @pl.when(step == 0)
    def _():
        for s in range(n_seq):
            for c in range(8):
                chip = place_ref[c]
                xr[c, s, 0:64] = x_ref[chip, s, mine]
                xr[c, s, 64:128] = x_ref[chip, s, others]
                xt[s, :, c * 128 : (c + 1) * 128] = xr[c, s].T
        acc[...] = jnp.zeros_like(acc)

    ones = jnp.ones((16, 1024), BF16)
    turns = own_ref.shape[1] // 2
    rounds = [(u, s) for u in range(turns) for s in range(n_seq)]
    blocks = [2 * (step * turns + u) for u in range(turns)]

    def score(n):
        u, s = rounds[n]
        block = blocks[u]
        xq = jnp.concatenate([x_ref[block, s].T, x_ref[block + 1, s].T], axis=1)
        rhs_q = jnp.concatenate([zeros(32), xq[0:32], zeros(64)], axis=0)
        top = jnp.full((8, iw), -jnp.inf, F32)
        k = 8
        for d in range(0, 8, k):
            big = nn(xr[d : d + k, s].reshape(k * 128, 128), rhs_q)
            for c in range(d, d + k):
                lo = jnp.concatenate([own_ref[c, 2 * u], other_ref[c, 2 * u]], axis=0)
                hi = jnp.concatenate([own_ref[c, 2 * u + 1], other_ref[c, 2 * u + 1]], axis=0)
                sc = big[(c - d) * 128 : (c - d + 1) * 128]
                sc = sc + jnp.concatenate([lo, hi], axis=1).astype(F32)
                scores[n % 2, c] = sc
                top = jnp.maximum(top, jnp.max(sc.reshape(16, 8, iw), axis=0))
                yield
        return xq, rhs_q, jnp.max(top, axis=0, keepdims=True)

    def weigh(n, xq, top):
        u, s = rounds[n]
        for c in range(8):
            ed[n % 2, c, :, :iw] = jnp.exp(scores[n % 2, c] - top).astype(BF16)
            yield
        left = jnp.concatenate([xt[s, 64:96, :], ones], axis=0)
        ot = nn(left, ed[n % 2, :, :, :iw].reshape(1024, iw))
        inv = 1.0 / ot[32:33]
        ot = ot[0:32] * inv
        da = (xq[96:128].astype(F32) * inv).astype(BF16)
        delta = jnp.sum(da.astype(F32) * ot, axis=0, keepdims=True)
        rhs_a = jnp.concatenate([zeros(64), da, zeros(32)], axis=0)
        return ot, rhs_a, delta

    def back(n, rhs_q, rhs_a, delta, ot):
        u, s = rounds[n]
        block = blocks[u]
        k = 8
        for c in range(8):
            if c % k == 0:
                big = nn(xr[c : c + k, s].reshape(k * 128, 128), rhs_a)
            e = ed[n % 2, c, :, :iw]
            ds = e.astype(F32) * (big[c % k * 128 : (c % k + 1) * 128] - delta)
            low = ds.astype(BF16)
            ed[n % 2, c, :, iw:] = low
            if s == 0:
                total[c] = ds
            elif s < n_seq - 1:
                total[c] += ds
            else:
                low = (total[c] + ds).astype(BF16)
                for t in range(2):
                    down_ref[c, 2 * u + t] = low[:64, t * 128 : (t + 1) * 128]
                    dother_ref[c, 2 * u + t] = low[64:, t * 128 : (t + 1) * 128]
            if (c + 1) % 8 == 0:
                w = slice(c + 1 - 8, c + 1)
                both = jnp.concatenate([rhs_a, rhs_q], axis=1)
                more = nt(ed[n % 2, w].reshape(8 * 128, 2 * iw), both)
                acc[s, w] += more.reshape(8, 128, 128)
            yield
        dq = nn(xt[s, 32:64, :], ed[n % 2, :, :, iw:].reshape(1024, iw)) * SCALE
        both = jnp.concatenate([ot, jnp.zeros((64, iw), F32), dq], axis=0)
        for t in range(2):
            qd[s, block + t] = both[:, t * 128 : (t + 1) * 128].T

    state = {}

    def drive(gens):
        live = list(gens)
        while live:
            for item in list(live):
                key, gen = item
                try:
                    next(gen)
                except StopIteration as stop:
                    state[key] = stop.value
                    live.remove(item)

    for t in range(len(rounds) + 2):
        gens = []
        if 0 <= t - 1 < len(rounds):
            xq, rhs_q, top = state["s", t - 1]
            gens.append((("w", t - 1), weigh(t - 1, xq, top)))
        if t < len(rounds):
            gens.append((("s", t), score(t)))
        if t >= 2:
            xq, rhs_q, top = state["s", t - 2]
            ot, rhs_a, delta = state["w", t - 2]
            gens.append((("b", t - 2), back(t - 2, rhs_q, rhs_a, delta, ot)))
        drive(gens)

    @pl.when(step == pl.num_programs(0) - 1)
    def _():
        for s in range(n_seq):
            for c in range(8):
                chip = place_ref[c]
                o_ref[chip, s, mine] = (acc[s, c, 0:64] + qd[s, chip, mine]).astype(BF16)
                o_ref[chip, s, others] = (acc[s, c, 64:128] + qd[s, chip, others]).astype(BF16)


def attention(place, x, own, other):
    r, s, n, _ = x.shape
    half = pl.BlockSpec((8, 4, 64, 128), lambda g, p: (0, g, 0, 0))
    whole = pl.BlockSpec((r, s, n, 128), lambda g, p: (0, 0, 0, 0))
    return pl.pallas_call(
        attention_kernel,
        grid_spec=pltpu.PrefetchScalarGridSpec(
            num_scalar_prefetch=1,
            grid=(2,),
            in_specs=[whole, half, half],
            out_specs=[whole, half, half],
            scratch_shapes=[
                pltpu.VMEM((r, s, n, 128), BF16),
                pltpu.VMEM((s, 128, 1024), BF16),
                pltpu.VMEM((s, 8, 128, 128), F32),
                pltpu.VMEM((s, 8, 128, 128), F32),
                pltpu.VMEM((2, 8, 128, 256), F32),
                pltpu.VMEM((2, 8, 128, 512), BF16),
                pltpu.VMEM((8, 128, 256), F32),
            ],
        ),
        out_shape=[
            jax.ShapeDtypeStruct((r, s, n, 128), BF16),
            jax.ShapeDtypeStruct((8, r, 64, 128), BF16),
            jax.ShapeDtypeStruct((8, r, 64, 128), BF16),
        ],
        compiler_params=params(),
        cost_estimate=cost(18),
        name="attention",
    )(place, x, own, other)


def finish_kernel(
    place_ref, x_ref, gain_ref, w_ref, wo_ref, up_ref, gate_ref, dg_ref, back_ref,
    inc_ref, dx_ref, keep_ref, away_ref, acc,
):
    step = pl.program_id(0)
    seqs, rows, width = x_ref.shape
    flat = lambda ref: ref[...].reshape(seqs * rows, width)
    hat, inv = normalize(flat(x_ref))
    gain = gain_ref[...]
    normed = (hat * gain).astype(BF16)
    gate = flat(gate_ref)
    d_gated = flat(dg_ref)
    up = flat(up_ref)
    back = [back_ref[h].reshape(seqs * rows, 128) for h in range(HEADS)]
    pick = lambda a: jnp.concatenate([b[:, a * DH : (a + 1) * DH] for b in back], axis=1)
    attended = pick(0).astype(F32)
    gated = (gate * attended).astype(BF16)
    inc_ref[...] = nn(gated, wo_ref[...]).astype(BF16).reshape(seqs, rows, width)
    d_pre = (d_gated * attended * gate * (1.0 - gate)).astype(BF16)
    d_proj = jnp.concatenate([pick(3), pick(1), pick(2), d_pre], axis=1)
    grad = nt(d_proj, w_ref[...])
    grad = normalize_grad(hat, inv, gain, grad).astype(BF16)
    dx_ref[...] = grad.reshape(seqs, rows, width)

    @pl.when(step == 0)
    def _():
        acc[...] = jnp.zeros_like(acc)

    acc[:, :1024] += tn(normed, d_proj)
    acc[:, 1024:] += tn(gated, up)

    last = step == pl.num_programs(0) - 1
    core = place_ref[8]

    def write(low_ref, high_ref):
        for b in range(5):
            low_ref[b] = acc[:, b * 128 : (b + 1) * 128].astype(BF16)
            high_ref[b] = acc[:, (b + 5) * 128 : (b + 6) * 128].astype(BF16)

    @pl.when(jnp.logical_and(last, core == 0))
    def _():
        write(keep_ref, away_ref)

    @pl.when(jnp.logical_and(last, core != 0))
    def _():
        write(away_ref, keep_ref)


def finish(place, x, gain, w, wo, up, gate, dg, back):
    s, n, c = x.shape
    whole = lambda *shape: pl.BlockSpec(shape, lambda i, p: (0,) * len(shape))
    row = pl.BlockSpec((2, n, c), lambda i, p: (i, 0, 0))
    return pl.pallas_call(
        finish_kernel,
        grid_spec=pltpu.PrefetchScalarGridSpec(
            num_scalar_prefetch=1,
            grid=(s // 2,),
            in_specs=[
                row, whole(1, c), whole(c, 4 * c), whole(c, c), row, row, row,
                pl.BlockSpec((HEADS, 2, n, 128), lambda i, p: (0, i, 0, 0)),
            ],
            out_specs=[row, row, whole(5, 256, 128), whole(5, 256, 128)],
            scratch_shapes=[pltpu.VMEM((c, 5 * c), F32)],
        ),
        out_shape=[
            jax.ShapeDtypeStruct((s, n, c), BF16),
            jax.ShapeDtypeStruct((s, n, c), BF16),
            jax.ShapeDtypeStruct((5, 256, 128), BF16),
            jax.ShapeDtypeStruct((5, 256, 128), BF16),
        ],
        compiler_params=params(),
        cost_estimate=cost(5),
        name="finish",
    )(place, x, gain, w, wo, up, gate, dg, back)


def pair_weight_kernel(n_ref, db_ref, dw_ref, tmp):
    tmp[...] = db_ref[0].astype(F32) + db_ref[1].astype(F32)
    total = jnp.zeros((HEADS, 128), F32)
    for j in range(n_ref.shape[0]):
        total = total + nn(tmp[:, j, :].astype(BF16), n_ref[j])

    @pl.when(pl.program_id(0) == 0)
    def _():
        dw_ref[...] = total

    @pl.when(pl.program_id(0) > 0)
    def _():
        dw_ref[...] += total


def pair_weight(normed, db):
    j, i, c = normed.shape
    step = 32
    return pl.pallas_call(
        pair_weight_kernel,
        grid=(j // step,),
        in_specs=[
            pl.BlockSpec((step, i, c), lambda g: (g, 0, 0)),
            pl.BlockSpec((2, HEADS, step, i), lambda g: (0, 0, g, 0)),
        ],
        out_specs=pl.BlockSpec((HEADS, c), lambda g: (0, 0)),
        out_shape=jax.ShapeDtypeStruct((HEADS, c), F32),
        scratch_shapes=[pltpu.VMEM((HEADS, step, i), F32)],
        compiler_params=params(),
        cost_estimate=cost(2),
        name="pair_weight",
    )(normed, db)


def pair_grad_kernel(x_ref, gain_ref, wt_ref, db_ref, dx_ref, spread):
    step = pl.program_id(0)
    gain = gain_ref[...]
    rows = x_ref.shape[0]
    ones = jnp.full((128, 128), 1 / 128, BF16)

    @pl.when(step == 0)
    def _():
        place = lax.broadcasted_iota(jnp.int32, (HEADS, rows, 128), 1)
        weight = wt_ref[...].astype(F32) * gain
        mean = jnp.broadcast_to(jnp.mean(weight, axis=1, keepdims=True), (HEADS, 128))
        parts = []
        for value in (weight, mean):
            high = value.astype(BF16).astype(F32)
            parts.append((high, value - high))
        for j in range(rows):
            for t in range(2):
                for k in range(2):
                    wide = jnp.broadcast_to(parts[t][k][:, None, :], (HEADS, rows, 128))
                    block = jnp.where(place == j, wide, 0.0).reshape(HEADS * rows, 128)
                    spread[j, k * 128 : (k + 1) * 128, t * 128 : (t + 1) * 128] = block.astype(
                        BF16
                    )

    db = db_ref[0].astype(F32) + db_ref[1].astype(F32)
    turned = db.reshape(HEADS * rows, 128).T.astype(BF16)
    turned = jnp.concatenate([turned, turned], axis=1)
    hat, inv = normalize_pairs(x_ref[...].reshape(rows * 128, 128), ones)
    both = [nn(turned, spread[j]) for j in range(rows)]
    grad = jnp.concatenate([b[:, :128] for b in both], axis=0)
    mean = jnp.concatenate([b[:, 128:] for b in both], axis=0)
    out = inv * (grad - mean - hat * row_mean(grad * hat, ones))
    dx_ref[...] = out.astype(BF16).reshape(rows, 128, 128)


def pair_grad(pair, gain, wt, db, begun=None):
    j, i, c = pair.shape
    step = 16
    half = j // step // 2
    first = 0 if begun is None else half
    more = () if begun is None else (begun,)
    body = lambda x, g, w, b, *rest: pair_grad_kernel(x, g, w, b, *rest[-2:])
    return pl.pallas_call(
        body,
        grid=(half,),
        in_specs=[
            pl.BlockSpec((step, i, c), lambda g: (g + first, 0, 0)),
            pl.BlockSpec((1, c), lambda g: (0, 0)),
            pl.BlockSpec((HEADS, c), lambda g: (0, 0)),
            pl.BlockSpec((2, HEADS, step, i), lambda g: (0, 0, g + first, 0)),
        ]
        + [pl.BlockSpec(memory_space=pl.ANY)] * len(more),
        out_specs=pl.BlockSpec((step, i, c), lambda g: (g + first, 0, 0)),
        out_shape=jax.ShapeDtypeStruct((j, i, c), BF16),
        scratch_shapes=[pltpu.VMEM((step, 2 * HEADS * step, 256), BF16)],
        input_output_aliases={4: 0} if more else {},
        compiler_params=params(),
        cost_estimate=cost(4),
        name="pair_grad",
    )(pair, gain, wt, db, *more)


def swap(x, axis):
    return lax.all_to_all(x, axis, split_axis=0, concat_axis=0, tiled=True)


OTHER = [(i, i ^ 1) for i in range(16)]


def along(shift):
    move = lambda i: (i & 9) | (((((i >> 1) & 3) + shift) % 4) << 1)
    return [(i, move(i)) for i in range(16)]


def send(x, pairs):
    return lax.ppermute(x, "seq", pairs)


def chip_order():
    me = lax.axis_index("seq")
    z, core = (me >> 1) & 3, me & 1
    chips = [d * 4 + ((z - shift) & 3) for shift in range(4) for d in range(2)]
    return jnp.stack(chips + [core]).astype(jnp.int32)


def device(far, low, z, x, core):
    return (far * 8 + z * 2 + core) * 8 + x * 2 + low


LAYERS = [
    [device(far, low, z, x, core) for z in range(4) for x in range(4)]
    for far in range(2)
    for low in range(2)
    for core in range(2)
]
ALL = ("seq", "res")


COLUMNS = [
    [(far * 8 + line) * 8 + res for far in range(2) for res in range(8)] for line in range(8)
]


def group_swap(x, groups):
    return lax.all_to_all(
        x, ALL, split_axis=0, concat_axis=0, tiled=True, axis_index_groups=groups
    )


def across(k):
    pairs = []
    for i in range(128):
        seq, res = divmod(i, 8)
        pairs.append((i, (seq ^ ((k >> 1) * 8)) * 8 + (res ^ (k & 1))))
    return pairs


def sum_layers(part, extra):
    part = jnp.sum(part.astype(F32), axis=0)
    part = jnp.concatenate([part, jnp.pad(extra, ((0, 8), (0, 0)))])
    low = part.astype(BF16)
    for k in (1, 2, 3):
        part = part + lax.ppermute(low, ALL, across(k)).astype(F32)
    part = part.astype(BF16)
    return group_swap(jnp.broadcast_to(part[None], (16,) + part.shape), LAYERS)


def unpack_kernel(place_ref, mine_ref, other_ref, dw_ref, dwo_ref, dwb_ref):
    dwb_ref[...] = sum(
        ref[i, 80:96].astype(F32) for ref in (mine_ref, other_ref) for i in range(16)
    )[0:8]

    def write(low, high):
        get = lambda ref, b: jnp.concatenate(
            [ref[i, lo:hi].astype(F32) for i, lo, hi in block_rows(b)], axis=0
        )
        for b in range(10):
            block = get(low, b) if b < 5 else get(high, b - 5)
            if b < 8:
                dw_ref[:, b * 128 : (b + 1) * 128] = block
            else:
                dwo_ref[:, (b - 8) * 128 : (b - 7) * 128] = block

    @pl.when(place_ref[8] == 0)
    def _():
        write(mine_ref, other_ref)

    @pl.when(place_ref[8] != 0)
    def _():
        write(other_ref, mine_ref)


def block_rows(b):
    pieces = []
    row = b * 256
    while row < (b + 1) * 256:
        i, lo = divmod(row, 80)
        hi = min(80, lo + (b + 1) * 256 - row)
        pieces.append((i, lo, hi))
        row += hi - lo
    return pieces


def unpack(place, mine, other):
    fixed = lambda *shape: pl.BlockSpec(shape, lambda g, p: (0,) * len(shape))
    return pl.pallas_call(
        unpack_kernel,
        grid_spec=pltpu.PrefetchScalarGridSpec(
            num_scalar_prefetch=1,
            grid=(1,),
            in_specs=[fixed(16, 96, 128)] * 2,
            out_specs=[fixed(256, 1024), fixed(256, 256), fixed(8, 128)],
        ),
        out_shape=[
            jax.ShapeDtypeStruct((256, 1024), F32),
            jax.ShapeDtypeStruct((256, 256), F32),
            jax.ShapeDtypeStruct((8, 128), F32),
        ],
        compiler_params=params(16),
        cost_estimate=cost(1),
        name="unpack",
    )(place, mine, other)


def local(x, gain, w, shift, wo, pair, pair_gain, wb, up):
    gain = gain.reshape(1, -1)
    shift = shift.reshape(1, -1)
    pair_gain = pair_gain.reshape(1, -1)
    wt = wb.T
    place = chip_order()
    bias, normed = pair_bias(pair, pair_gain, wt)
    couple = group_swap(bias.reshape(16, 64, 128), COLUMNS).reshape(2, 8, 64, 128)
    packed, gate, dg = project(x, gain, w, shift, wo, up)
    couple, packed = lax.optimization_barrier((couple, packed))
    heads = swap(packed, "res")
    own = jnp.concatenate([couple] + [send(couple, along(turn)) for turn in (1, 2, 3)])
    own, heads = lax.optimization_barrier((own, heads))
    other = send(own, OTHER)
    back, d_own, d_other = attention(place, heads, own, other)
    back = swap(back, "res")
    low = (d_own.astype(F32) + send(d_other, OTHER).astype(F32)).astype(BF16)
    total = low[0:2].astype(F32)
    for turn in (1, 2, 3):
        total = total + send(low[2 * turn : 2 * turn + 2], along(-turn)).astype(F32)
    d_bias = group_swap(total.astype(BF16).reshape(16, 64, 128), COLUMNS).reshape(2, 8, 64, 128)
    inc, dx, keep, away = finish(place, x, gain, w, wo, up, gate, dg, back)
    d_bias, away = lax.optimization_barrier((d_bias, away))
    part = (keep.astype(F32) + send(away, OTHER).astype(F32)).astype(BF16)
    part = part.reshape(16, 80, 128)
    dwb = pair_weight(normed, d_bias)
    part = group_swap(part, LAYERS)
    begun = pair_grad(pair, pair_gain, wt, d_bias)
    part, begun = lax.optimization_barrier((part, begun))
    mine = sum_layers(part, dwb)
    d_pair = pair_grad(pair, pair_gain, wt, d_bias, begun)
    mine, d_pair = lax.optimization_barrier((mine, d_pair))
    dw, dwo, dwb = unpack(place, mine, send(mine, OTHER))
    return inc, dx, d_pair, dw, dwo, dwb.T


def solution(mesh):
    tok = P("seq", "res", None)
    return jax.shard_map(
        local,
        mesh=mesh,
        in_specs=(tok, P(), P(), P(), P(), tok, P(), P(), tok),
        out_specs=(tok, tok, tok, P(), P(), P()),
        check_vma=False,
    )
```

```python
import functools

import jax
import jax.numpy as jnp
from jax import lax
from jax.experimental import pallas as pl
from jax.experimental.pallas import tpu as pltpu
from jax.sharding import PartitionSpec as P

EPS = 1e-05
F32 = jnp.float32
BF16 = jnp.bfloat16
HEADS = 8
DH = 32
SCALE = DH ** (-0.5)


def nn(a, b):
    return lax.dot_general(a, b, (((1,), (0,)), ((), ())), preferred_element_type=F32)


def nt(a, b):
    return lax.dot_general(a, b, (((1,), (1,)), ((), ())), preferred_element_type=F32)


def tn(a, b):
    return lax.dot_general(a, b, (((0,), (0,)), ((), ())), preferred_element_type=F32)


def normalize(x):
    x = x.astype(F32)
    centered = x - jnp.mean(x, axis=-1, keepdims=True)
    inv = lax.rsqrt(jnp.mean(centered * centered, axis=-1, keepdims=True) + EPS)
    return centered * inv, inv


def normalize_grad(hat, inv, gain, grad):
    g = grad * gain
    mean_g = jnp.mean(g, axis=-1, keepdims=True)
    mean_gx = jnp.mean(g * hat, axis=-1, keepdims=True)
    return inv * (g - mean_g - hat * mean_gx)


def row_mean(x, ones):
    return nn(x.astype(BF16), ones)


def normalize_pairs(x, ones):
    centered = x.astype(F32) - nn(x, ones)
    inv = lax.rsqrt(row_mean(centered * centered, ones) + EPS)
    return centered * inv, inv


def cost(us):
    return pl.CostEstimate(flops=int(us * 1e9), bytes_accessed=int(us * 3e6), transcendentals=0)


def params(megabytes=60):
    return pltpu.CompilerParams(
        dimension_semantics=("arbitrary",), vmem_limit_bytes=megabytes * 1024 * 1024
    )


def project_kernel(x_ref, gain_ref, w_ref, shift_ref, wo_ref, up_ref, pack_ref, gate_ref, dg_ref):
    seqs, rows, width = x_ref.shape
    flat = lambda ref: ref[...].reshape(seqs * rows, width)
    hat, _ = normalize(flat(x_ref))
    normed = (hat * gain_ref[...]).astype(BF16)
    proj = nn(normed, w_ref[...])
    q = (proj[:, :256] * SCALE).astype(BF16)
    k = proj[:, 256:512].astype(BF16)
    v = proj[:, 512:768].astype(BF16)
    gate = jax.nn.sigmoid(proj[:, 768:] + shift_ref[...])
    d_gated = nt(flat(up_ref), wo_ref[...])
    da = (d_gated * gate).astype(BF16)
    gate_ref[...] = gate.reshape(seqs, rows, width)
    dg_ref[...] = d_gated.reshape(seqs, rows, width)
    for h in range(HEADS):
        c = slice(h * DH, (h + 1) * DH)
        packed = jnp.concatenate([q[:, c], k[:, c], v[:, c], da[:, c]], axis=1)
        pack_ref[h] = packed.reshape(seqs, rows, 128)


def project(x, gain, w, shift, wo, up):
    s, n, c = x.shape
    whole = lambda *shape: pl.BlockSpec(shape, lambda i: (0,) * len(shape))
    row = pl.BlockSpec((2, n, c), lambda i: (i, 0, 0))
    return pl.pallas_call(
        project_kernel,
        grid=(s // 2,),
        in_specs=[row, whole(1, c), whole(c, 4 * c), whole(1, c), whole(c, c), row],
        out_specs=[pl.BlockSpec((HEADS, 2, n, 128), lambda i: (0, i, 0, 0)), row, row],
        out_shape=[
            jax.ShapeDtypeStruct((HEADS, s, n, 128), BF16),
            jax.ShapeDtypeStruct((s, n, c), F32),
            jax.ShapeDtypeStruct((s, n, c), F32),
        ],
        compiler_params=params(),
        cost_estimate=cost(3),
        name="project",
    )(x, gain, w, shift, wo, up)


def bias_kernel(x_ref, gain_ref, wt_ref, out_ref, normed_ref, tmp):
    ones = jnp.full((128, 128), 1 / 128, BF16)
    rows = x_ref.shape[0]
    hat, _ = normalize_pairs(x_ref[...].reshape(rows * 128, 128), ones)
    normed = (hat * gain_ref[...]).astype(BF16).reshape(rows, 128, 128)
    normed_ref[...] = normed
    flat = nt(wt_ref[...], normed.reshape(rows * 128, 128))
    for j in range(rows):
        tmp[:, j, :] = flat[:, j * 128 : (j + 1) * 128]
    low = tmp[...].astype(BF16)
    out_ref[0] = low
    out_ref[1] = low


def pair_bias(pair, gain, wt):
    j, i, c = pair.shape
    step = 32
    return pl.pallas_call(
        bias_kernel,
        grid=(j // step,),
        in_specs=[
            pl.BlockSpec((step, i, c), lambda g: (g, 0, 0)),
            pl.BlockSpec((1, c), lambda g: (0, 0)),
            pl.BlockSpec((HEADS, c), lambda g: (0, 0)),
        ],
        out_specs=[
            pl.BlockSpec((2, HEADS, step, i), lambda g: (0, 0, g, 0)),
            pl.BlockSpec((step, i, c), lambda g: (g, 0, 0)),
        ],
        out_shape=[
            jax.ShapeDtypeStruct((2, HEADS, j, i), BF16),
            jax.ShapeDtypeStruct((j, i, c), BF16),
        ],
        scratch_shapes=[pltpu.VMEM((HEADS, step, i), F32)],
        compiler_params=params(),
        cost_estimate=cost(4),
        name="pair_bias",
    )(pair, gain, wt)


def attention_kernel(
    place_ref, x_ref, own_ref, other_ref, o_ref, down_ref, dother_ref,
    xr, xt, acc, qd, scores, ed, total,
):
    step = pl.program_id(0)
    n_seq = x_ref.shape[1]
    iw = 256
    core = place_ref[8]
    mine = pl.ds(pl.multiple_of(core * 64, 64), 64)
    others = pl.ds(pl.multiple_of((1 - core) * 64, 64), 64)
    zeros = lambda rows: jnp.zeros((rows, iw), BF16)

    @pl.when(step == 0)
    def _():
        for s in range(n_seq):
            for c in range(8):
                chip = place_ref[c]
                xr[c, s, 0:64] = x_ref[chip, s, mine]
                xr[c, s, 64:128] = x_ref[chip, s, others]
                xt[s, :, c * 128 : (c + 1) * 128] = xr[c, s].T
        acc[...] = jnp.zeros_like(acc)

    ones = jnp.ones((16, 1024), BF16)
    turns = own_ref.shape[1] // 2
    rounds = [(u, s) for u in range(turns) for s in range(n_seq)]
    blocks = [2 * (step * turns + u) for u in range(turns)]

    def score(n):
        u, s = rounds[n]
        block = blocks[u]
        xq = jnp.concatenate([x_ref[block, s].T, x_ref[block + 1, s].T], axis=1)
        rhs_q = jnp.concatenate([zeros(32), xq[0:32], zeros(64)], axis=0)
        top = jnp.full((8, iw), -jnp.inf, F32)
        k = 8
        for d in range(0, 8, k):
            big = nn(xr[d : d + k, s].reshape(k * 128, 128), rhs_q)
            for c in range(d, d + k):
                lo = jnp.concatenate([own_ref[c, 2 * u], other_ref[c, 2 * u]], axis=0)
                hi = jnp.concatenate([own_ref[c, 2 * u + 1], other_ref[c, 2 * u + 1]], axis=0)
                sc = big[(c - d) * 128 : (c - d + 1) * 128]
                sc = sc + jnp.concatenate([lo, hi], axis=1).astype(F32)
                scores[n % 2, c] = sc
                top = jnp.maximum(top, jnp.max(sc.reshape(16, 8, iw), axis=0))
                yield
        return xq, rhs_q, jnp.max(top, axis=0, keepdims=True)

    def weigh(n, xq, top):
        u, s = rounds[n]
        for c in range(8):
            ed[n % 2, c, :, :iw] = jnp.exp(scores[n % 2, c] - top).astype(BF16)
            yield
        left = jnp.concatenate([xt[s, 64:96, :], ones], axis=0)
        ot = nn(left, ed[n % 2, :, :, :iw].reshape(1024, iw))
        inv = 1.0 / ot[32:33]
        ot = ot[0:32] * inv
        da = (xq[96:128].astype(F32) * inv).astype(BF16)
        delta = jnp.sum(da.astype(F32) * ot, axis=0, keepdims=True)
        rhs_a = jnp.concatenate([zeros(64), da, zeros(32)], axis=0)
        return ot, rhs_a, delta

    def back(n, rhs_q, rhs_a, delta, ot):
        u, s = rounds[n]
        block = blocks[u]
        k = 8
        for c in range(8):
            if c % k == 0:
                big = nn(xr[c : c + k, s].reshape(k * 128, 128), rhs_a)
            e = ed[n % 2, c, :, :iw]
            ds = e.astype(F32) * (big[c % k * 128 : (c % k + 1) * 128] - delta)
            low = ds.astype(BF16)
            ed[n % 2, c, :, iw:] = low
            if s == 0:
                total[c] = ds
            elif s < n_seq - 1:
                total[c] += ds
            else:
                low = (total[c] + ds).astype(BF16)
                for t in range(2):
                    down_ref[c, 2 * u + t] = low[:64, t * 128 : (t + 1) * 128]
                    dother_ref[c, 2 * u + t] = low[64:, t * 128 : (t + 1) * 128]
            if (c + 1) % 8 == 0:
                w = slice(c + 1 - 8, c + 1)
                both = jnp.concatenate([rhs_a, rhs_q], axis=1)
                more = nt(ed[n % 2, w].reshape(8 * 128, 2 * iw), both)
                acc[s, w] += more.reshape(8, 128, 128)
            yield
        dq = nn(xt[s, 32:64, :], ed[n % 2, :, :, iw:].reshape(1024, iw)) * SCALE
        both = jnp.concatenate([ot, jnp.zeros((64, iw), F32), dq], axis=0)
        for t in range(2):
            qd[s, block + t] = both[:, t * 128 : (t + 1) * 128].T

    state = {}

    def drive(gens):
        live = list(gens)
        while live:
            for item in list(live):
                key, gen = item
                try:
                    next(gen)
                except StopIteration as stop:
                    state[key] = stop.value
                    live.remove(item)

    for t in range(len(rounds) + 2):
        gens = []
        if 0 <= t - 1 < len(rounds):
            xq, rhs_q, top = state["s", t - 1]
            gens.append((("w", t - 1), weigh(t - 1, xq, top)))
        if t < len(rounds):
            gens.append((("s", t), score(t)))
        if t >= 2:
            xq, rhs_q, top = state["s", t - 2]
            ot, rhs_a, delta = state["w", t - 2]
            gens.append((("b", t - 2), back(t - 2, rhs_q, rhs_a, delta, ot)))
        drive(gens)

    @pl.when(step == pl.num_programs(0) - 1)
    def _():
        for s in range(n_seq):
            for c in range(8):
                chip = place_ref[c]
                o_ref[chip, s, mine] = (acc[s, c, 0:64] + qd[s, chip, mine]).astype(BF16)
                o_ref[chip, s, others] = (acc[s, c, 64:128] + qd[s, chip, others]).astype(BF16)


def attention(place, x, own, other):
    r, s, n, _ = x.shape
    half = pl.BlockSpec((8, 4, 64, 128), lambda g, p: (0, g, 0, 0))
    whole = pl.BlockSpec((r, s, n, 128), lambda g, p: (0, 0, 0, 0))
    return pl.pallas_call(
        attention_kernel,
        grid_spec=pltpu.PrefetchScalarGridSpec(
            num_scalar_prefetch=1,
            grid=(2,),
            in_specs=[whole, half, half],
            out_specs=[whole, half, half],
            scratch_shapes=[
                pltpu.VMEM((r, s, n, 128), BF16),
                pltpu.VMEM((s, 128, 1024), BF16),
                pltpu.VMEM((s, 8, 128, 128), F32),
                pltpu.VMEM((s, 8, 128, 128), F32),
                pltpu.VMEM((2, 8, 128, 256), F32),
                pltpu.VMEM((2, 8, 128, 512), BF16),
                pltpu.VMEM((8, 128, 256), F32),
            ],
        ),
        out_shape=[
            jax.ShapeDtypeStruct((r, s, n, 128), BF16),
            jax.ShapeDtypeStruct((8, r, 64, 128), BF16),
            jax.ShapeDtypeStruct((8, r, 64, 128), BF16),
        ],
        compiler_params=params(),
        cost_estimate=cost(18),
        name="attention",
    )(place, x, own, other)


def finish_kernel(
    place_ref, x_ref, gain_ref, up_ref, gate_ref, dg_ref, back_ref,
    proj_ref, gated_ref, keep_ref, away_ref, acc,
):
    step = pl.program_id(0)
    seqs, rows, width = x_ref.shape
    flat = lambda ref: ref[...].reshape(seqs * rows, width)
    hat, _ = normalize(flat(x_ref))
    normed = (hat * gain_ref[...]).astype(BF16)
    gate = flat(gate_ref)
    d_gated = flat(dg_ref)
    up = flat(up_ref)
    back = [back_ref[h].reshape(seqs * rows, 128) for h in range(HEADS)]
    pick = lambda a: jnp.concatenate([b[:, a * DH : (a + 1) * DH] for b in back], axis=1)
    attended = pick(0).astype(F32)
    gated = (gate * attended).astype(BF16)
    gated_ref[...] = gated.reshape(seqs, rows, width)
    d_pre = (d_gated * attended * gate * (1.0 - gate)).astype(BF16)
    d_proj = jnp.concatenate([pick(3), pick(1), pick(2), d_pre], axis=1)
    proj_ref[...] = d_proj.reshape(seqs, rows, 4 * width)

    @pl.when(step == 0)
    def _():
        acc[...] = jnp.zeros_like(acc)

    acc[:, :1024] += tn(normed, d_proj)
    acc[:, 1024:] += tn(gated, up)

    last = step == pl.num_programs(0) - 1
    core = place_ref[8]

    def write(low_ref, high_ref):
        for b in range(5):
            low_ref[b] = acc[:, b * 128 : (b + 1) * 128].astype(BF16)
            high_ref[b] = acc[:, (b + 5) * 128 : (b + 6) * 128].astype(BF16)

    @pl.when(jnp.logical_and(last, core == 0))
    def _():
        write(keep_ref, away_ref)

    @pl.when(jnp.logical_and(last, core != 0))
    def _():
        write(away_ref, keep_ref)


def finish(place, x, gain, up, gate, dg, back):
    s, n, c = x.shape
    whole = lambda *shape: pl.BlockSpec(shape, lambda i, p: (0,) * len(shape))
    row = pl.BlockSpec((2, n, c), lambda i, p: (i, 0, 0))
    return pl.pallas_call(
        finish_kernel,
        grid_spec=pltpu.PrefetchScalarGridSpec(
            num_scalar_prefetch=1,
            grid=(s // 2,),
            in_specs=[
                row, whole(1, c), row, row, row,
                pl.BlockSpec((HEADS, 2, n, 128), lambda i, p: (0, i, 0, 0)),
            ],
            out_specs=[
                pl.BlockSpec((2, n, 4 * c), lambda i, p: (i, 0, 0)),
                row, whole(5, 256, 128), whole(5, 256, 128),
            ],
            scratch_shapes=[pltpu.VMEM((c, 5 * c), F32)],
        ),
        out_shape=[
            jax.ShapeDtypeStruct((s, n, 4 * c), BF16),
            jax.ShapeDtypeStruct((s, n, c), BF16),
            jax.ShapeDtypeStruct((5, 256, 128), BF16),
            jax.ShapeDtypeStruct((5, 256, 128), BF16),
        ],
        compiler_params=params(),
        cost_estimate=cost(5),
        name="finish",
    )(place, x, gain, up, gate, dg, back)


def input_kernel(x_ref, gain_ref, w_ref, wo_ref, proj_ref, gated_ref, inc_ref, dx_ref):
    seqs, rows, width = x_ref.shape
    flat = lambda ref: ref[...].reshape(seqs * rows, ref.shape[-1])
    inc_ref[...] = nn(flat(gated_ref), wo_ref[...]).astype(BF16).reshape(x_ref.shape)
    hat, inv = normalize(flat(x_ref))
    grad = nt(flat(proj_ref), w_ref[...])
    grad = normalize_grad(hat, inv, gain_ref[...], grad).astype(BF16)
    dx_ref[...] = grad.reshape(x_ref.shape)


def input_grad(x, gain, w, wo, d_proj, gated):
    s, n, c = x.shape
    whole = lambda *shape: pl.BlockSpec(shape, lambda i: (0,) * len(shape))
    row = pl.BlockSpec((2, n, c), lambda i: (i, 0, 0))
    return pl.pallas_call(
        input_kernel,
        grid=(s // 2,),
        in_specs=[
            row, whole(1, c), whole(c, 4 * c), whole(c, c),
            pl.BlockSpec((2, n, 4 * c), lambda i: (i, 0, 0)), row,
        ],
        out_specs=[row, row],
        out_shape=[jax.ShapeDtypeStruct((s, n, c), BF16)] * 2,
        compiler_params=params(),
        cost_estimate=cost(3),
        name="input_grad",
    )(x, gain, w, wo, d_proj, gated)


def pair_weight_kernel(n_ref, db_ref, dw_ref, tmp):
    tmp[...] = db_ref[0].astype(F32) + db_ref[1].astype(F32)
    rows = n_ref.shape[0]
    left = jnp.concatenate([tmp[:, j, :].astype(BF16) for j in range(rows)], axis=1)
    total = nn(left, n_ref[...].reshape(rows * 128, 128))

    @pl.when(pl.program_id(0) == 0)
    def _():
        dw_ref[...] = total

    @pl.when(pl.program_id(0) > 0)
    def _():
        dw_ref[...] += total


def pair_weight(normed, db):
    j, i, c = normed.shape
    step = 32
    return pl.pallas_call(
        pair_weight_kernel,
        grid=(j // step,),
        in_specs=[
            pl.BlockSpec((step, i, c), lambda g: (g, 0, 0)),
            pl.BlockSpec((2, HEADS, step, i), lambda g: (0, 0, g, 0)),
        ],
        out_specs=pl.BlockSpec((HEADS, c), lambda g: (0, 0)),
        out_shape=jax.ShapeDtypeStruct((HEADS, c), F32),
        scratch_shapes=[pltpu.VMEM((HEADS, step, i), F32)],
        compiler_params=params(),
        cost_estimate=cost(2),
        name="pair_weight",
    )(normed, db)


def pair_grad_kernel(x_ref, gain_ref, wt_ref, db_ref, dx_ref, spread):
    step = pl.program_id(0)
    gain = gain_ref[...]
    rows = x_ref.shape[0]
    ones = jnp.full((128, 128), 1 / 128, BF16)

    @pl.when(step == 0)
    def _():
        place = lax.broadcasted_iota(jnp.int32, (HEADS, rows, 128), 1)
        weight = wt_ref[...].astype(F32) * gain
        mean = jnp.broadcast_to(jnp.mean(weight, axis=1, keepdims=True), (HEADS, 128))
        parts = []
        for value in (weight, mean):
            high = value.astype(BF16).astype(F32)
            parts.append((high, value - high))
        for j in range(rows):
            for t in range(2):
                for k in range(2):
                    wide = jnp.broadcast_to(parts[t][k][:, None, :], (HEADS, rows, 128))
                    block = jnp.where(place == j, wide, 0.0).reshape(HEADS * rows, 128)
                    spread[j, k * 128 : (k + 1) * 128, t * 128 : (t + 1) * 128] = block.astype(
                        BF16
                    )

    db = db_ref[0].astype(F32) + db_ref[1].astype(F32)
    turned = db.reshape(HEADS * rows, 128).T.astype(BF16)
    turned = jnp.concatenate([turned, turned], axis=1)
    hat, inv = normalize_pairs(x_ref[...].reshape(rows * 128, 128), ones)
    both = [nn(turned, spread[j]) for j in range(rows)]
    grad = jnp.concatenate([b[:, :128] for b in both], axis=0)
    mean = jnp.concatenate([b[:, 128:] for b in both], axis=0)
    out = inv * (grad - mean - hat * row_mean(grad * hat, ones))
    dx_ref[...] = out.astype(BF16).reshape(rows, 128, 128)


def pair_grad(pair, gain, wt, db, begun=None):
    j, i, c = pair.shape
    step = 16
    half = j // step // 2
    first = 0 if begun is None else half
    more = () if begun is None else (begun,)
    body = lambda x, g, w, b, *rest: pair_grad_kernel(x, g, w, b, *rest[-2:])
    return pl.pallas_call(
        body,
        grid=(half,),
        in_specs=[
            pl.BlockSpec((step, i, c), lambda g: (g + first, 0, 0)),
            pl.BlockSpec((1, c), lambda g: (0, 0)),
            pl.BlockSpec((HEADS, c), lambda g: (0, 0)),
            pl.BlockSpec((2, HEADS, step, i), lambda g: (0, 0, g + first, 0)),
        ]
        + [pl.BlockSpec(memory_space=pl.ANY)] * len(more),
        out_specs=pl.BlockSpec((step, i, c), lambda g: (g + first, 0, 0)),
        out_shape=jax.ShapeDtypeStruct((j, i, c), BF16),
        scratch_shapes=[pltpu.VMEM((step, 2 * HEADS * step, 256), BF16)],
        input_output_aliases={4: 0} if more else {},
        compiler_params=params(),
        cost_estimate=cost(4),
        name="pair_grad",
    )(pair, gain, wt, db, *more)


def swap(x, axis):
    return lax.all_to_all(x, axis, split_axis=0, concat_axis=0, tiled=True)


OTHER = [(i, i ^ 1) for i in range(16)]


def along(shift):
    move = lambda i: (i & 9) | (((((i >> 1) & 3) + shift) % 4) << 1)
    return [(i, move(i)) for i in range(16)]


def send(x, pairs):
    return lax.ppermute(x, "seq", pairs)


def chip_order():
    me = lax.axis_index("seq")
    z, core = (me >> 1) & 3, me & 1
    chips = [d * 4 + ((z - shift) & 3) for shift in range(4) for d in range(2)]
    return jnp.stack(chips + [core]).astype(jnp.int32)


def device(far, low, z, x, core):
    return (far * 8 + z * 2 + core) * 8 + x * 2 + low


LAYERS = [
    [device(far, low, z, x, core) for z in range(4) for x in range(4)]
    for far in range(2)
    for low in range(2)
    for core in range(2)
]
ALL = ("seq", "res")


COLUMNS = [
    [(far * 8 + line) * 8 + res for far in range(2) for res in range(8)] for line in range(8)
]


def group_swap(x, groups):
    return lax.all_to_all(
        x, ALL, split_axis=0, concat_axis=0, tiled=True, axis_index_groups=groups
    )


def across(k):
    pairs = []
    for i in range(128):
        seq, res = divmod(i, 8)
        pairs.append((i, (seq ^ ((k >> 1) * 8)) * 8 + (res ^ (k & 1))))
    return pairs


def add_kernel(a_ref, b_ref, out_ref):
    out_ref[...] = (a_ref[...].astype(F32) + b_ref[...].astype(F32)).astype(BF16)


def add_halves(a, b):
    return pl.pallas_call(
        add_kernel,
        out_shape=jax.ShapeDtypeStruct(a.shape, BF16),
        compiler_params=pltpu.CompilerParams(vmem_limit_bytes=8 * 1024 * 1024),
        cost_estimate=cost(1),
        name="add_halves",
    )(a, b)


def spread_kernel(a_ref, b_ref, c_ref, d_ref, out_ref):
    near = a_ref[...].astype(F32) + b_ref[...].astype(F32)
    far = c_ref[...].astype(F32) + d_ref[...].astype(F32)
    total = (near + far).astype(BF16)
    for i in range(out_ref.shape[0]):
        out_ref[i] = total


def spread_sum(*parts):
    return pl.pallas_call(
        spread_kernel,
        out_shape=jax.ShapeDtypeStruct((16,) + parts[0].shape, BF16),
        compiler_params=pltpu.CompilerParams(vmem_limit_bytes=8 * 1024 * 1024),
        cost_estimate=cost(1),
        name="spread_sum",
    )(*parts)


def sum_layers(part, extra):
    part = jnp.sum(part.astype(F32), axis=0)
    part = jnp.concatenate([part, jnp.pad(extra, ((0, 8), (0, 0)))])
    low = part.astype(BF16)
    parts = [low] + [lax.ppermute(low, ALL, across(k)) for k in (1, 2, 3)]
    return group_swap(spread_sum(*parts), LAYERS)


def unpack_kernel(place_ref, mine_ref, other_ref, dw_ref, dwo_ref, dwb_ref):
    column = lambda ref: sum(ref[i, 80:96].astype(F32) for i in range(16))
    dwb_ref[...] = (column(mine_ref) + column(other_ref))[0:8]

    def write(low, high):
        get = lambda ref, b: jnp.concatenate(
            [ref[i, lo:hi].astype(F32) for i, lo, hi in block_rows(b)], axis=0
        )
        for b in range(10):
            block = get(low, b) if b < 5 else get(high, b - 5)
            if b < 8:
                dw_ref[:, b * 128 : (b + 1) * 128] = block
            else:
                dwo_ref[:, (b - 8) * 128 : (b - 7) * 128] = block

    @pl.when(place_ref[8] == 0)
    def _():
        write(mine_ref, other_ref)

    @pl.when(place_ref[8] != 0)
    def _():
        write(other_ref, mine_ref)


def block_rows(b):
    pieces = []
    row = b * 256
    while row < (b + 1) * 256:
        i, lo = divmod(row, 80)
        hi = min(80, lo + (b + 1) * 256 - row)
        pieces.append((i, lo, hi))
        row += hi - lo
    return pieces


def unpack(place, mine, other):
    fixed = lambda *shape: pl.BlockSpec(shape, lambda g, p: (0,) * len(shape))
    return pl.pallas_call(
        unpack_kernel,
        grid_spec=pltpu.PrefetchScalarGridSpec(
            num_scalar_prefetch=1,
            grid=(1,),
            in_specs=[fixed(16, 96, 128)] * 2,
            out_specs=[fixed(256, 1024), fixed(256, 256), fixed(8, 128)],
        ),
        out_shape=[
            jax.ShapeDtypeStruct((256, 1024), F32),
            jax.ShapeDtypeStruct((256, 256), F32),
            jax.ShapeDtypeStruct((8, 128), F32),
        ],
        compiler_params=params(16),
        cost_estimate=cost(1),
        name="unpack",
    )(place, mine, other)


def local(x, gain, w, shift, wo, pair, pair_gain, wb, up):
    gain = gain.reshape(1, -1)
    shift = shift.reshape(1, -1)
    pair_gain = pair_gain.reshape(1, -1)
    wt = wb.T
    place = chip_order()
    bias, normed = pair_bias(pair, pair_gain, wt)
    couple = group_swap(bias.reshape(16, 64, 128), COLUMNS).reshape(2, 8, 64, 128)
    packed, gate, dg = project(x, gain, w, shift, wo, up)
    couple, packed = lax.optimization_barrier((couple, packed))
    heads = swap(packed, "res")
    own = jnp.concatenate([couple] + [send(couple, along(turn)) for turn in (1, 2, 3)])
    own, heads = lax.optimization_barrier((own, heads))
    other = send(own, OTHER)
    back, d_own, d_other = attention(place, heads, own, other)
    back = swap(back, "res")
    low = (d_own.astype(F32) + send(d_other, OTHER).astype(F32)).astype(BF16)
    total = low[0:2].astype(F32)
    for turn in (1, 2, 3):
        total = total + send(low[2 * turn : 2 * turn + 2], along(-turn)).astype(F32)
    d_bias = group_swap(total.astype(BF16).reshape(16, 64, 128), COLUMNS).reshape(2, 8, 64, 128)
    d_proj, gated, keep, away = finish(place, x, gain, up, gate, dg, back)
    d_bias, away = lax.optimization_barrier((d_bias, away))
    part = add_halves(keep, send(away, OTHER)).reshape(16, 80, 128)
    dwb = pair_weight(normed, d_bias)
    part = group_swap(part, LAYERS)
    begun = pair_grad(pair, pair_gain, wt, d_bias)
    part, begun = lax.optimization_barrier((part, begun))
    mine = sum_layers(part, dwb)
    d_pair = pair_grad(pair, pair_gain, wt, d_bias, begun)
    inc, dx = input_grad(x, gain, w, wo, d_proj, gated)
    mine, d_pair, inc, dx = lax.optimization_barrier((mine, d_pair, inc, dx))
    dw, dwo, dwb = unpack(place, mine, send(mine, OTHER))
    return inc, dx, d_pair, dw, dwo, dwb.T


def solution(mesh):
    tok = P("seq", "res", None)
    return jax.shard_map(
        local,
        mesh=mesh,
        in_specs=(tok, P(), P(), P(), P(), tok, P(), P(), tok),
        out_specs=(tok, tok, tok, P(), P(), P()),
        check_vma=False,
    )
```

```python
import functools

import jax
import jax.numpy as jnp
from jax import lax
from jax.experimental import pallas as pl
from jax.experimental.pallas import tpu as pltpu
from jax.sharding import PartitionSpec as P

EPS = 1e-05
F32 = jnp.float32
BF16 = jnp.bfloat16
HEADS = 8
DH = 32
SCALE = DH ** (-0.5)


def nn(a, b):
    return lax.dot_general(a, b, (((1,), (0,)), ((), ())), preferred_element_type=F32)


def nt(a, b):
    return lax.dot_general(a, b, (((1,), (1,)), ((), ())), preferred_element_type=F32)


def tn(a, b):
    return lax.dot_general(a, b, (((0,), (0,)), ((), ())), preferred_element_type=F32)


def normalize(x):
    x = x.astype(F32)
    centered = x - jnp.mean(x, axis=-1, keepdims=True)
    inv = lax.rsqrt(jnp.mean(centered * centered, axis=-1, keepdims=True) + EPS)
    return centered * inv, inv


def normalize_grad(hat, inv, gain, grad):
    g = grad * gain
    mean_g = jnp.mean(g, axis=-1, keepdims=True)
    mean_gx = jnp.mean(g * hat, axis=-1, keepdims=True)
    return inv * (g - mean_g - hat * mean_gx)


def row_mean(x, ones):
    return nn(x.astype(BF16), ones)


def normalize_pairs(x, ones):
    centered = x.astype(F32) - nn(x, ones)
    inv = lax.rsqrt(row_mean(centered * centered, ones) + EPS)
    return centered * inv, inv


def cost(us):
    return pl.CostEstimate(flops=int(us * 1e9), bytes_accessed=int(us * 3e6), transcendentals=0)


def params(megabytes=60):
    return pltpu.CompilerParams(
        dimension_semantics=("arbitrary",), vmem_limit_bytes=megabytes * 1024 * 1024
    )


def project_kernel(x_ref, gain_ref, w_ref, shift_ref, wo_ref, up_ref, pack_ref, gate_ref, dg_ref):
    seqs, rows, width = x_ref.shape
    flat = lambda ref: ref[...].reshape(seqs * rows, width)
    hat, _ = normalize(flat(x_ref))
    normed = (hat * gain_ref[...]).astype(BF16)
    proj = nn(normed, w_ref[...])
    q = (proj[:, :256] * SCALE).astype(BF16)
    k = proj[:, 256:512].astype(BF16)
    v = proj[:, 512:768].astype(BF16)
    gate = jax.nn.sigmoid(proj[:, 768:] + shift_ref[...])
    d_gated = nt(flat(up_ref), wo_ref[...])
    da = (d_gated * gate).astype(BF16)
    gate_ref[...] = gate.reshape(seqs, rows, width)
    dg_ref[...] = d_gated.reshape(seqs, rows, width)
    for h in range(HEADS):
        c = slice(h * DH, (h + 1) * DH)
        packed = jnp.concatenate([q[:, c], k[:, c], v[:, c], da[:, c]], axis=1)
        pack_ref[h] = packed.reshape(seqs, rows, 128)


def project(x, gain, w, shift, wo, up):
    s, n, c = x.shape
    whole = lambda *shape: pl.BlockSpec(shape, lambda i: (0,) * len(shape))
    row = pl.BlockSpec((2, n, c), lambda i: (i, 0, 0))
    return pl.pallas_call(
        project_kernel,
        grid=(s // 2,),
        in_specs=[row, whole(1, c), whole(c, 4 * c), whole(1, c), whole(c, c), row],
        out_specs=[pl.BlockSpec((HEADS, 2, n, 128), lambda i: (0, i, 0, 0)), row, row],
        out_shape=[
            jax.ShapeDtypeStruct((HEADS, s, n, 128), BF16),
            jax.ShapeDtypeStruct((s, n, c), F32),
            jax.ShapeDtypeStruct((s, n, c), F32),
        ],
        compiler_params=params(),
        cost_estimate=cost(3),
        name="project",
    )(x, gain, w, shift, wo, up)


def bias_kernel(x_ref, gain_ref, wt_ref, out_ref, normed_ref, tmp):
    ones = jnp.full((128, 128), 1 / 128, BF16)
    rows = x_ref.shape[0]
    hat, _ = normalize_pairs(x_ref[...].reshape(rows * 128, 128), ones)
    normed = (hat * gain_ref[...]).astype(BF16).reshape(rows, 128, 128)
    normed_ref[...] = normed
    flat = nt(wt_ref[...], normed.reshape(rows * 128, 128))
    for j in range(rows):
        tmp[:, j, :] = flat[:, j * 128 : (j + 1) * 128]
    low = tmp[...].astype(BF16)
    out_ref[0] = low
    out_ref[1] = low


def pair_bias(pair, gain, wt):
    j, i, c = pair.shape
    step = 32
    return pl.pallas_call(
        bias_kernel,
        grid=(j // step,),
        in_specs=[
            pl.BlockSpec((step, i, c), lambda g: (g, 0, 0)),
            pl.BlockSpec((1, c), lambda g: (0, 0)),
            pl.BlockSpec((HEADS, c), lambda g: (0, 0)),
        ],
        out_specs=[
            pl.BlockSpec((2, HEADS, step, i), lambda g: (0, 0, g, 0)),
            pl.BlockSpec((step, i, c), lambda g: (g, 0, 0)),
        ],
        out_shape=[
            jax.ShapeDtypeStruct((2, HEADS, j, i), BF16),
            jax.ShapeDtypeStruct((j, i, c), BF16),
        ],
        scratch_shapes=[pltpu.VMEM((HEADS, step, i), F32)],
        compiler_params=params(),
        cost_estimate=cost(4),
        name="pair_bias",
    )(pair, gain, wt)


def attention_kernel(
    place_ref, x_ref, own_ref, other_ref, o_ref, down_ref, dother_ref,
    xr, xt, acc, qd, scores, ed, total,
):
    step = pl.program_id(0)
    n_seq = x_ref.shape[1]
    iw = 256
    core = place_ref[8]
    mine = pl.ds(pl.multiple_of(core * 64, 64), 64)
    others = pl.ds(pl.multiple_of((1 - core) * 64, 64), 64)
    zeros = lambda rows: jnp.zeros((rows, iw), BF16)

    @pl.when(step == 0)
    def _():
        for s in range(n_seq):
            for c in range(8):
                chip = place_ref[c]
                xr[c, s, 0:64] = x_ref[chip, s, mine]
                xr[c, s, 64:128] = x_ref[chip, s, others]
                xt[s, :, c * 128 : (c + 1) * 128] = xr[c, s].T
        acc[...] = jnp.zeros_like(acc)

    ones = jnp.ones((16, 1024), BF16)
    turns = own_ref.shape[1] // 2
    rounds = [(u, s) for u in range(turns) for s in range(n_seq)]
    blocks = [2 * (step * turns + u) for u in range(turns)]

    def score(n):
        u, s = rounds[n]
        block = blocks[u]
        xq = jnp.concatenate([x_ref[block, s].T, x_ref[block + 1, s].T], axis=1)
        rhs_q = jnp.concatenate([zeros(32), xq[0:32], zeros(64)], axis=0)
        top = jnp.full((8, iw), -jnp.inf, F32)
        k = 8
        for d in range(0, 8, k):
            big = nn(xr[d : d + k, s].reshape(k * 128, 128), rhs_q)
            for c in range(d, d + k):
                lo = jnp.concatenate([own_ref[c, 2 * u], other_ref[c, 2 * u]], axis=0)
                hi = jnp.concatenate([own_ref[c, 2 * u + 1], other_ref[c, 2 * u + 1]], axis=0)
                sc = big[(c - d) * 128 : (c - d + 1) * 128]
                sc = sc + jnp.concatenate([lo, hi], axis=1).astype(F32)
                scores[n % 2, c] = sc
                top = jnp.maximum(top, jnp.max(sc.reshape(16, 8, iw), axis=0))
                yield
        return xq, rhs_q, jnp.max(top, axis=0, keepdims=True)

    def weigh(n, xq, top):
        u, s = rounds[n]
        for c in range(8):
            ed[n % 2, c, :, :iw] = jnp.exp(scores[n % 2, c] - top).astype(BF16)
            yield
        left = jnp.concatenate([xt[s, 64:96, :], ones], axis=0)
        ot = nn(left, ed[n % 2, :, :, :iw].reshape(1024, iw))
        inv = 1.0 / ot[32:33]
        ot = ot[0:32] * inv
        da = (xq[96:128].astype(F32) * inv).astype(BF16)
        delta = jnp.sum(da.astype(F32) * ot, axis=0, keepdims=True)
        rhs_a = jnp.concatenate([zeros(64), da, zeros(32)], axis=0)
        return ot, rhs_a, delta

    def back(n, rhs_q, rhs_a, delta, ot):
        u, s = rounds[n]
        block = blocks[u]
        k = 8
        for c in range(8):
            if c % k == 0:
                big = nn(xr[c : c + k, s].reshape(k * 128, 128), rhs_a)
            e = ed[n % 2, c, :, :iw]
            ds = e.astype(F32) * (big[c % k * 128 : (c % k + 1) * 128] - delta)
            low = ds.astype(BF16)
            ed[n % 2, c, :, iw:] = low
            if s == 0:
                total[c] = ds
            elif s < n_seq - 1:
                total[c] += ds
            else:
                low = (total[c] + ds).astype(BF16)
                for t in range(2):
                    down_ref[c, 2 * u + t] = low[:64, t * 128 : (t + 1) * 128]
                    dother_ref[c, 2 * u + t] = low[64:, t * 128 : (t + 1) * 128]
            if (c + 1) % 8 == 0:
                w = slice(c + 1 - 8, c + 1)
                both = jnp.concatenate([rhs_a, rhs_q], axis=1)
                more = nt(ed[n % 2, w].reshape(8 * 128, 2 * iw), both)
                acc[s, w] += more.reshape(8, 128, 128)
            yield
        dq = nn(xt[s, 32:64, :], ed[n % 2, :, :, iw:].reshape(1024, iw)) * SCALE
        both = jnp.concatenate([ot, jnp.zeros((64, iw), F32), dq], axis=0)
        for t in range(2):
            qd[s, block + t] = both[:, t * 128 : (t + 1) * 128].T

    state = {}

    def drive(gens):
        live = list(gens)
        while live:
            for item in list(live):
                key, gen = item
                try:
                    next(gen)
                except StopIteration as stop:
                    state[key] = stop.value
                    live.remove(item)

    for t in range(len(rounds) + 2):
        gens = []
        if 0 <= t - 1 < len(rounds):
            xq, rhs_q, top = state["s", t - 1]
            gens.append((("w", t - 1), weigh(t - 1, xq, top)))
        if t < len(rounds):
            gens.append((("s", t), score(t)))
        if t >= 2:
            xq, rhs_q, top = state["s", t - 2]
            ot, rhs_a, delta = state["w", t - 2]
            gens.append((("b", t - 2), back(t - 2, rhs_q, rhs_a, delta, ot)))
        drive(gens)

    @pl.when(step == pl.num_programs(0) - 1)
    def _():
        for s in range(n_seq):
            for c in range(8):
                chip = place_ref[c]
                o_ref[chip, s, mine] = (acc[s, c, 0:64] + qd[s, chip, mine]).astype(BF16)
                o_ref[chip, s, others] = (acc[s, c, 64:128] + qd[s, chip, others]).astype(BF16)


def attention(place, x, own, other):
    r, s, n, _ = x.shape
    half = pl.BlockSpec((8, 8, 64, 128), lambda g, p: (0, g, 0, 0))
    whole = pl.BlockSpec((r, s, n, 128), lambda g, p: (0, 0, 0, 0))
    return pl.pallas_call(
        attention_kernel,
        grid_spec=pltpu.PrefetchScalarGridSpec(
            num_scalar_prefetch=1,
            grid=(1,),
            in_specs=[whole, half, half],
            out_specs=[whole, half, half],
            scratch_shapes=[
                pltpu.VMEM((r, s, n, 128), BF16),
                pltpu.VMEM((s, 128, 1024), BF16),
                pltpu.VMEM((s, 8, 128, 128), F32),
                pltpu.VMEM((s, 8, 128, 128), F32),
                pltpu.VMEM((2, 8, 128, 256), F32),
                pltpu.VMEM((2, 8, 128, 512), BF16),
                pltpu.VMEM((8, 128, 256), F32),
            ],
        ),
        out_shape=[
            jax.ShapeDtypeStruct((r, s, n, 128), BF16),
            jax.ShapeDtypeStruct((8, r, 64, 128), BF16),
            jax.ShapeDtypeStruct((8, r, 64, 128), BF16),
        ],
        compiler_params=params(),
        cost_estimate=cost(18),
        name="attention",
    )(place, x, own, other)


def finish_kernel(
    place_ref, x_ref, gain_ref, w_ref, wo_ref, up_ref, gate_ref, dg_ref, back_ref,
    inc_ref, dx_ref, keep_ref, away_ref, acc,
):
    step = pl.program_id(0)
    seqs, rows, width = x_ref.shape
    flat = lambda ref: ref[...].reshape(seqs * rows, width)
    hat, inv = normalize(flat(x_ref))
    gain = gain_ref[...]
    normed = (hat * gain).astype(BF16)
    gate = flat(gate_ref)
    d_gated = flat(dg_ref)
    up = flat(up_ref)
    back = [back_ref[h].reshape(seqs * rows, 128) for h in range(HEADS)]
    pick = lambda a: jnp.concatenate([b[:, a * DH : (a + 1) * DH] for b in back], axis=1)
    attended = pick(0).astype(F32)
    gated = (gate * attended).astype(BF16)
    inc_ref[...] = nn(gated, wo_ref[...]).astype(BF16).reshape(seqs, rows, width)
    d_pre = (d_gated * attended * gate * (1.0 - gate)).astype(BF16)
    d_proj = jnp.concatenate([pick(3), pick(1), pick(2), d_pre], axis=1)
    grad = nt(d_proj, w_ref[...])
    grad = normalize_grad(hat, inv, gain, grad).astype(BF16)
    dx_ref[...] = grad.reshape(seqs, rows, width)

    @pl.when(step == 0)
    def _():
        acc[...] = jnp.zeros_like(acc)

    acc[:, :1024] += tn(normed, d_proj)
    acc[:, 1024:] += tn(gated, up)

    last = step == pl.num_programs(0) - 1
    core = place_ref[8]

    def write(low_ref, high_ref):
        for b in range(5):
            low_ref[b] = acc[:, b * 128 : (b + 1) * 128].astype(BF16)
            high_ref[b] = acc[:, (b + 5) * 128 : (b + 6) * 128].astype(BF16)

    @pl.when(jnp.logical_and(last, core == 0))
    def _():
        write(keep_ref, away_ref)

    @pl.when(jnp.logical_and(last, core != 0))
    def _():
        write(away_ref, keep_ref)


def finish(place, x, gain, w, wo, up, gate, dg, back):
    s, n, c = x.shape
    whole = lambda *shape: pl.BlockSpec(shape, lambda i, p: (0,) * len(shape))
    row = pl.BlockSpec((2, n, c), lambda i, p: (i, 0, 0))
    return pl.pallas_call(
        finish_kernel,
        grid_spec=pltpu.PrefetchScalarGridSpec(
            num_scalar_prefetch=1,
            grid=(s // 2,),
            in_specs=[
                row, whole(1, c), whole(c, 4 * c), whole(c, c), row, row, row,
                pl.BlockSpec((HEADS, 2, n, 128), lambda i, p: (0, i, 0, 0)),
            ],
            out_specs=[row, row, whole(5, 256, 128), whole(5, 256, 128)],
            scratch_shapes=[pltpu.VMEM((c, 5 * c), F32)],
        ),
        out_shape=[
            jax.ShapeDtypeStruct((s, n, c), BF16),
            jax.ShapeDtypeStruct((s, n, c), BF16),
            jax.ShapeDtypeStruct((5, 256, 128), BF16),
            jax.ShapeDtypeStruct((5, 256, 128), BF16),
        ],
        compiler_params=params(),
        cost_estimate=cost(5),
        name="finish",
    )(place, x, gain, w, wo, up, gate, dg, back)


def pair_weight_kernel(n_ref, db_ref, dw_ref, tmp):
    tmp[...] = db_ref[0].astype(F32) + db_ref[1].astype(F32)
    total = jnp.zeros((HEADS, 128), F32)
    for j in range(n_ref.shape[0]):
        total = total + nn(tmp[:, j, :].astype(BF16), n_ref[j])

    @pl.when(pl.program_id(0) == 0)
    def _():
        dw_ref[...] = total

    @pl.when(pl.program_id(0) > 0)
    def _():
        dw_ref[...] += total


def pair_weight(normed, db):
    j, i, c = normed.shape
    step = 32
    return pl.pallas_call(
        pair_weight_kernel,
        grid=(j // step,),
        in_specs=[
            pl.BlockSpec((step, i, c), lambda g: (g, 0, 0)),
            pl.BlockSpec((2, HEADS, step, i), lambda g: (0, 0, g, 0)),
        ],
        out_specs=pl.BlockSpec((HEADS, c), lambda g: (0, 0)),
        out_shape=jax.ShapeDtypeStruct((HEADS, c), F32),
        scratch_shapes=[pltpu.VMEM((HEADS, step, i), F32)],
        compiler_params=params(),
        cost_estimate=cost(2),
        name="pair_weight",
    )(normed, db)


def pair_grad_kernel(x_ref, gain_ref, wt_ref, db_ref, dx_ref, spread):
    step = pl.program_id(0)
    gain = gain_ref[...]
    rows = x_ref.shape[0]
    ones = jnp.full((128, 128), 1 / 128, BF16)

    @pl.when(step == 0)
    def _():
        place = lax.broadcasted_iota(jnp.int32, (HEADS, rows, 128), 1)
        weight = wt_ref[...].astype(F32) * gain
        mean = jnp.broadcast_to(jnp.mean(weight, axis=1, keepdims=True), (HEADS, 128))
        parts = []
        for value in (weight, mean):
            high = value.astype(BF16).astype(F32)
            parts.append((high, value - high))
        for j in range(rows):
            for t in range(2):
                for k in range(2):
                    wide = jnp.broadcast_to(parts[t][k][:, None, :], (HEADS, rows, 128))
                    block = jnp.where(place == j, wide, 0.0).reshape(HEADS * rows, 128)
                    spread[j, k * 128 : (k + 1) * 128, t * 128 : (t + 1) * 128] = block.astype(
                        BF16
                    )

    db = db_ref[0].astype(F32) + db_ref[1].astype(F32)
    turned = db.reshape(HEADS * rows, 128).T.astype(BF16)
    turned = jnp.concatenate([turned, turned], axis=1)
    hat, inv = normalize_pairs(x_ref[...].reshape(rows * 128, 128), ones)
    both = [nn(turned, spread[j]) for j in range(rows)]
    grad = jnp.concatenate([b[:, :128] for b in both], axis=0)
    mean = jnp.concatenate([b[:, 128:] for b in both], axis=0)
    out = inv * (grad - mean - hat * row_mean(grad * hat, ones))
    dx_ref[...] = out.astype(BF16).reshape(rows, 128, 128)


def pair_grad(pair, gain, wt, db, begun=None):
    j, i, c = pair.shape
    step = 16
    half = j // step // 2
    first = 0 if begun is None else half
    more = () if begun is None else (begun,)
    body = lambda x, g, w, b, *rest: pair_grad_kernel(x, g, w, b, *rest[-2:])
    return pl.pallas_call(
        body,
        grid=(half,),
        in_specs=[
            pl.BlockSpec((step, i, c), lambda g: (g + first, 0, 0)),
            pl.BlockSpec((1, c), lambda g: (0, 0)),
            pl.BlockSpec((HEADS, c), lambda g: (0, 0)),
            pl.BlockSpec((2, HEADS, step, i), lambda g: (0, 0, g + first, 0)),
        ]
        + [pl.BlockSpec(memory_space=pl.ANY)] * len(more),
        out_specs=pl.BlockSpec((step, i, c), lambda g: (g + first, 0, 0)),
        out_shape=jax.ShapeDtypeStruct((j, i, c), BF16),
        scratch_shapes=[pltpu.VMEM((step, 2 * HEADS * step, 256), BF16)],
        input_output_aliases={4: 0} if more else {},
        compiler_params=params(),
        cost_estimate=cost(4),
        name="pair_grad",
    )(pair, gain, wt, db, *more)


def swap(x, axis):
    return lax.all_to_all(x, axis, split_axis=0, concat_axis=0, tiled=True)


OTHER = [(i, i ^ 1) for i in range(16)]


def along(shift):
    move = lambda i: (i & 9) | (((((i >> 1) & 3) + shift) % 4) << 1)
    return [(i, move(i)) for i in range(16)]


def send(x, pairs):
    return lax.ppermute(x, "seq", pairs)


def chip_order():
    me = lax.axis_index("seq")
    z, core = (me >> 1) & 3, me & 1
    chips = [d * 4 + ((z - shift) & 3) for shift in range(4) for d in range(2)]
    return jnp.stack(chips + [core]).astype(jnp.int32)


def device(far, low, z, x, core):
    return (far * 8 + z * 2 + core) * 8 + x * 2 + low


LAYERS = [
    [device(far, low, z, x, core) for z in range(4) for x in range(4)]
    for far in range(2)
    for low in range(2)
    for core in range(2)
]
ALL = ("seq", "res")


COLUMNS = [
    [(far * 8 + line) * 8 + res for far in range(2) for res in range(8)] for line in range(8)
]


def group_swap(x, groups):
    return lax.all_to_all(
        x, ALL, split_axis=0, concat_axis=0, tiled=True, axis_index_groups=groups
    )


def across(k):
    pairs = []
    for i in range(128):
        seq, res = divmod(i, 8)
        pairs.append((i, (seq ^ ((k >> 1) * 8)) * 8 + (res ^ (k & 1))))
    return pairs


def sum_layers(part, extra):
    part = jnp.sum(part.astype(F32), axis=0)
    part = jnp.concatenate([part, jnp.pad(extra, ((0, 8), (0, 0)))])
    low = part.astype(BF16)
    near, far, last = [lax.ppermute(low, ALL, across(k)).astype(F32) for k in (1, 2, 3)]
    part = ((low.astype(F32) + near) + (far + last)).astype(BF16)
    return group_swap(jnp.broadcast_to(part[None], (16,) + part.shape), LAYERS)


def unpack_kernel(place_ref, mine_ref, other_ref, dw_ref, dwo_ref, dwb_ref):
    column = lambda ref: sum(ref[i, 80:96].astype(F32) for i in range(16))
    dwb_ref[...] = (column(mine_ref) + column(other_ref))[0:8]

    def write(low, high):
        get = lambda ref, b: jnp.concatenate(
            [ref[i, lo:hi].astype(F32) for i, lo, hi in block_rows(b)], axis=0
        )
        for b in range(10):
            block = get(low, b) if b < 5 else get(high, b - 5)
            if b < 8:
                dw_ref[:, b * 128 : (b + 1) * 128] = block
            else:
                dwo_ref[:, (b - 8) * 128 : (b - 7) * 128] = block

    @pl.when(place_ref[8] == 0)
    def _():
        write(mine_ref, other_ref)

    @pl.when(place_ref[8] != 0)
    def _():
        write(other_ref, mine_ref)


def block_rows(b):
    pieces = []
    row = b * 256
    while row < (b + 1) * 256:
        i, lo = divmod(row, 80)
        hi = min(80, lo + (b + 1) * 256 - row)
        pieces.append((i, lo, hi))
        row += hi - lo
    return pieces


def unpack(place, mine, other):
    fixed = lambda *shape: pl.BlockSpec(shape, lambda g, p: (0,) * len(shape))
    return pl.pallas_call(
        unpack_kernel,
        grid_spec=pltpu.PrefetchScalarGridSpec(
            num_scalar_prefetch=1,
            grid=(1,),
            in_specs=[fixed(16, 96, 128)] * 2,
            out_specs=[fixed(256, 1024), fixed(256, 256), fixed(8, 128)],
        ),
        out_shape=[
            jax.ShapeDtypeStruct((256, 1024), F32),
            jax.ShapeDtypeStruct((256, 256), F32),
            jax.ShapeDtypeStruct((8, 128), F32),
        ],
        compiler_params=params(16),
        cost_estimate=cost(1),
        name="unpack",
    )(place, mine, other)


def local(x, gain, w, shift, wo, pair, pair_gain, wb, up):
    gain = gain.reshape(1, -1)
    shift = shift.reshape(1, -1)
    pair_gain = pair_gain.reshape(1, -1)
    wt = wb.T
    place = chip_order()
    bias, normed = pair_bias(pair, pair_gain, wt)
    couple = group_swap(bias.reshape(16, 64, 128), COLUMNS).reshape(2, 8, 64, 128)
    packed, gate, dg = project(x, gain, w, shift, wo, up)
    couple, packed = lax.optimization_barrier((couple, packed))
    heads = swap(packed, "res")
    own = jnp.concatenate([couple] + [send(couple, along(turn)) for turn in (1, 2, 3)])
    own, heads = lax.optimization_barrier((own, heads))
    other = send(own, OTHER)
    back, d_own, d_other = attention(place, heads, own, other)
    back = swap(back, "res")
    low = (d_own.astype(F32) + send(d_other, OTHER).astype(F32)).astype(BF16)
    total = low[0:2].astype(F32)
    for turn in (1, 2, 3):
        total = total + send(low[2 * turn : 2 * turn + 2], along(-turn)).astype(F32)
    d_bias = group_swap(total.astype(BF16).reshape(16, 64, 128), COLUMNS).reshape(2, 8, 64, 128)
    inc, dx, keep, away = finish(place, x, gain, w, wo, up, gate, dg, back)
    d_bias, away = lax.optimization_barrier((d_bias, away))
    part = (keep.astype(F32) + send(away, OTHER).astype(F32)).astype(BF16)
    part = part.reshape(16, 80, 128)
    dwb = pair_weight(normed, d_bias)
    part = group_swap(part, LAYERS)
    begun = pair_grad(pair, pair_gain, wt, d_bias)
    part, begun = lax.optimization_barrier((part, begun))
    mine = sum_layers(part, dwb)
    d_pair = pair_grad(pair, pair_gain, wt, d_bias, begun)
    mine, d_pair = lax.optimization_barrier((mine, d_pair))
    dw, dwo, dwb = unpack(place, mine, send(mine, OTHER))
    return inc, dx, d_pair, dw, dwo, dwb.T


def solution(mesh):
    tok = P("seq", "res", None)
    return jax.shard_map(
        local,
        mesh=mesh,
        in_specs=(tok, P(), P(), P(), P(), tok, P(), P(), tok),
        out_specs=(tok, tok, tok, P(), P(), P()),
        check_vma=False,
    )
```
